32 devices in a mesh: dp: 4 (over x, core), fsdp: 8 (over z, y).
Axes of the slice: x: 2, y: 2, z: 4, core: 2. Of those that a mesh axis runs over, the one named last changes fastest.
Arguments:
- attention_output_rows: bfloat16 [8192, 1536], P(('dp', 'fsdp')), may hold values from -6 to 6
- cotangent: bfloat16 [8192, 3072], P(('dp', 'fsdp')), may hold values from -6 to 6
- quantized_weight_codes: bfloat16 [1536, 3072], P('fsdp'), may hold values from -1 to 1
- shard_absolute_maximum: bfloat16 [8], P('fsdp'), may hold values from 0.019897461 to 0.079589844
- adapter_down_weight: bfloat16 [1536, 128], P('fsdp'), may hold values from -0.15625 to 0.15625
- adapter_up_weight: bfloat16 [128, 3072], P(None, 'fsdp'), may hold values from -0.5 to 0.5
- timestep_gate_weight: bfloat16 [256, 3072], P('fsdp'), may hold values from -0.375 to 0.375
- timesteps: int32 [2], replicated, may hold values from 0 to 999
Outputs:
- mixed_update: bfloat16 [8192, 3072], P(('dp', 'fsdp'))
- attention_output_gradient: bfloat16 [8192, 1536], P(('dp', 'fsdp'))
- down_grad: float32 [1536, 128], P('fsdp')
- scaled_up_gradient: float32 [128, 3072], P(None, 'fsdp')
The draws below stay inside these ranges and needn't reach their ends.
All inputs are finite; a program needn't handle non-finite values.
Results may differ from the reference program's by a relative error of at most 0.0075.
Values may be sent and summed in bfloat16 or wider, within the bound.
A program may use at most 64 MiB of HBM per device.

```python
import math
import jax
import jax.numpy as jnp

MODEL_WIDTH = 3072
INNER_FEATURES = 1536
ADAPTER_RANK = 128
FREQ = 256
PATCHES = 4096
TOKENS = 8192
SAMPLES = 2
N_FSDP = 8


def with_spikes(result, rng, source, target, parts, factor):
    def block_of(axis_at):
        return (jnp.arange(result.shape[axis_at]) // (result.shape[axis_at] // parts)).reshape((-1,) + (1,) * (result.ndim - 1 - axis_at))

    one_side = jax.random.permutation(rng, parts)[block_of(target)]
    other_side = (block_of(target) + parts // 2) % parts
    return jnp.where((block_of(source) == one_side) | (block_of(source) == other_side), factor * result, result)


def steps_of(key, extent, split, least, largest):
    def one(position, parts):
        steps = jax.random.uniform(jax.random.fold_in(jax.random.fold_in(key, 6), position), (parts,), jnp.float32, least / len(split), largest / len(split))
        return jnp.repeat(jnp.exp(steps), extent[position] // parts).reshape((-1,) + (1,) * (len(extent) - position - 1))

    loudness = one(*split[0])
    for cut in split[1:]:
        loudness = loudness * one(*cut)
    return loudness


def scatter_about(key, dims, deviation, reach, shards=(), kind=jnp.bfloat16):
    result = jax.random.normal(key, dims, jnp.float32) * deviation
    if len(shards) > 0:
        result = steps_of(key, dims, shards, -0.22, 0.18) * result
    return jnp.clip(result, min=-reach, max=reach).astype(kind)


def heavy_noise(own_key, shape, scale, bound, shards, heavy, kind=jnp.bfloat16):
    drawn = scale * jax.random.normal(own_key, shape, jnp.float32)
    if shards:
        drawn = drawn * steps_of(own_key, shape, shards, -0.22, 0.18)
    return jnp.clip(with_spikes(drawn, jax.random.fold_in(own_key, 3), *heavy), -bound, bound).astype(kind)


def setup_inputs(seed: int = 0) -> dict:
    splits = jax.random.split(jax.random.key(seed), 9)
    return {
        "attention_output_rows": heavy_noise(splits[0], (TOKENS, INNER_FEATURES), 1.0, 6.0, ((0, 32),), (0, 1, 32, 2.75)),
        "cotangent": heavy_noise(splits[1], (TOKENS, MODEL_WIDTH), 1.0, 6.0, ((0, 32),), (0, 1, 32, 2.75)),
        "quantized_weight_codes": jnp.clip(jax.random.uniform(splits[2], (INNER_FEATURES, MODEL_WIDTH), jnp.float32, -1.0, 1.0) * steps_of(splits[2], (INNER_FEATURES, MODEL_WIDTH), ((0, 8),), -0.4, 0.0), -1.0, 1.0).astype(jnp.bfloat16),
        "shard_absolute_maximum": jnp.clip(jnp.exp(math.log(0.079589844) - 1.3862944 * jax.random.uniform(splits[3], (N_FSDP,), jnp.float32) ** steps_of(splits[3], (N_FSDP,), ((0, 8),), -0.2, 0.2)), 0.019897461, 0.079589844).astype(jnp.bfloat16),
        "adapter_down_weight": scatter_about(splits[4], (INNER_FEATURES, ADAPTER_RANK), INNER_FEATURES ** -0.5, 0.15625, ((0, 8),)),
        "adapter_up_weight": scatter_about(splits[5], (ADAPTER_RANK, MODEL_WIDTH), ADAPTER_RANK ** -0.5, 0.5, ((1, 8),)),
        "timestep_gate_weight": scatter_about(splits[6], (FREQ, MODEL_WIDTH), FREQ ** -0.5, 0.375, ((0, 8),)),
        "timesteps": jax.random.randint(splits[7], (SAMPLES,), 0, 1000).astype(jnp.int32),
    }


adapter_scale_factor = 0.5


def reference(attention_output_rows, cotangent, quantized_weight_codes, shard_absolute_maximum, adapter_down_weight, adapter_up_weight, timestep_gate_weight, timesteps):
    shard_rows = INNER_FEATURES // N_FSDP
    amax_rows = jnp.repeat(shard_absolute_maximum.astype(jnp.float32), shard_rows)
    weight = (quantized_weight_codes.astype(jnp.float32) * amax_rows[:, None]).astype(jnp.bfloat16)
    half_freq = FREQ // 2
    frequency = jnp.exp(-math.log(10000.0) * jnp.arange(half_freq, dtype=jnp.float32) / half_freq)
    phase_angle = timesteps.astype(jnp.float32)[:, None] * frequency[None, :]
    features = jnp.concatenate([jnp.cos(phase_angle), jnp.sin(phase_angle)], axis=1).astype(jnp.bfloat16)
    gate_row = jnp.dot(features, timestep_gate_weight, preferred_element_type=jnp.float32)
    bottleneck_activation = jnp.dot(attention_output_rows, adapter_down_weight, preferred_element_type=jnp.float32).astype(jnp.bfloat16)
    projection_output = jnp.dot(attention_output_rows, weight, preferred_element_type=jnp.float32)
    projection_output = projection_output + adapter_scale_factor * jnp.dot(bottleneck_activation, adapter_up_weight, preferred_element_type=jnp.float32)
    mixed_update = (projection_output.reshape(SAMPLES, PATCHES, MODEL_WIDTH) * gate_row[:, None, :]).reshape(TOKENS, MODEL_WIDTH).astype(jnp.bfloat16)
    gated_branch_gradient = (cotangent.astype(jnp.float32).reshape(SAMPLES, PATCHES, MODEL_WIDTH) * gate_row[:, None, :]).reshape(TOKENS, MODEL_WIDTH).astype(jnp.bfloat16)
    bottleneck_gradient = (adapter_scale_factor * jnp.dot(gated_branch_gradient, adapter_up_weight.T, preferred_element_type=jnp.float32)).astype(jnp.bfloat16)
    attention_output_gradient = jnp.dot(gated_branch_gradient, weight.T, preferred_element_type=jnp.float32)
    attention_output_gradient = (attention_output_gradient + jnp.dot(bottleneck_gradient, adapter_down_weight.T, preferred_element_type=jnp.float32)).astype(jnp.bfloat16)
    gradient_scale_factor = TOKENS ** -0.5
    down_grad = jnp.dot(attention_output_rows.T, bottleneck_gradient, preferred_element_type=jnp.float32) * gradient_scale_factor
    scaled_up_gradient = jnp.dot(bottleneck_activation.T, gated_branch_gradient, preferred_element_type=jnp.float32) * (adapter_scale_factor * gradient_scale_factor)
    return mixed_update, attention_output_gradient, down_grad, scaled_up_gradient
```

```python
import functools
import math

import jax
import jax.numpy as jnp
from jax import lax
from jax.experimental import pallas as pl
from jax.experimental.pallas import tpu as pltpu
from jax.sharding import PartitionSpec as P

FREQ = 256
PATCHES = 4096


adapter_scale_factor = 0.5


def per_device(
    attention_output_rows,
    cotangent,
    quantized_weight_codes,
    shard_absolute_maximum,
    adapter_down_weight,
    adapter_up_weight,
    timestep_gate_weight,
    timesteps,
):
    row_count = attention_output_rows.shape[0]
    dp_count = lax.axis_size("dp")
    fsdp_count = lax.axis_size("fsdp")
    amax_rows = jnp.broadcast_to(shard_absolute_maximum, (quantized_weight_codes.shape[0],))
    all_codes, scales = (
        lax.all_gather(quantized_weight_codes, "fsdp", axis=0, tiled=True),
        lax.all_gather(amax_rows, "fsdp", axis=0, tiled=True),
    )
    weight = (all_codes.astype(jnp.float32) * scales.astype(jnp.float32)[:, None]).astype(
        jnp.bfloat16
    )
    down_all, gathered_up_weight, gate_all = (
        lax.all_gather(adapter_down_weight, "fsdp", axis=0, tiled=True),
        lax.all_gather(adapter_up_weight, "fsdp", axis=1, tiled=True),
        lax.all_gather(timestep_gate_weight, "fsdp", axis=0, tiled=True),
    )
    sample_index = (
        (lax.axis_index("dp") * fsdp_count + lax.axis_index("fsdp")) * row_count // PATCHES
    )
    step_value = lax.dynamic_slice_in_dim(timesteps, sample_index, 1)
    half_freq = FREQ // 2
    frequency = jnp.exp(-math.log(10000.0) * jnp.arange(half_freq, dtype=jnp.float32) / half_freq)
    phase_angle = step_value.astype(jnp.float32)[:, None] * frequency[None, :]
    features = jnp.concatenate([jnp.cos(phase_angle), jnp.sin(phase_angle)], axis=1).astype(
        jnp.bfloat16
    )
    gate_row = jnp.dot(features, gate_all, preferred_element_type=jnp.float32)
    bottleneck_activation = jnp.dot(
        attention_output_rows, down_all, preferred_element_type=jnp.float32
    ).astype(jnp.bfloat16)
    projection_output = jnp.dot(attention_output_rows, weight, preferred_element_type=jnp.float32)
    projection_output = projection_output + adapter_scale_factor * jnp.dot(
        bottleneck_activation, gathered_up_weight, preferred_element_type=jnp.float32
    )
    mixed_update = (projection_output * gate_row).astype(jnp.bfloat16)
    gated_branch_gradient = (cotangent.astype(jnp.float32) * gate_row).astype(jnp.bfloat16)
    bottleneck_gradient = (
        adapter_scale_factor
        * jnp.dot(gated_branch_gradient, gathered_up_weight.T, preferred_element_type=jnp.float32)
    ).astype(jnp.bfloat16)
    attention_output_gradient = jnp.dot(
        gated_branch_gradient, weight.T, preferred_element_type=jnp.float32
    )
    attention_output_gradient = (
        attention_output_gradient
        + jnp.dot(bottleneck_gradient, down_all.T, preferred_element_type=jnp.float32)
    ).astype(jnp.bfloat16)
    term_down = jnp.dot(
        attention_output_rows.T, bottleneck_gradient, preferred_element_type=jnp.float32
    )
    term_up = jnp.dot(
        bottleneck_activation.T, gated_branch_gradient, preferred_element_type=jnp.float32
    )
    gradient_scale_factor = (row_count * dp_count * fsdp_count) ** (-0.5)
    shard_terms = (
        lax.psum_scatter(term_down, "fsdp", scatter_dimension=0, tiled=True),
        lax.psum_scatter(term_up, "fsdp", scatter_dimension=1, tiled=True),
    )
    summed_down, reduced_up_gradient = lax.psum((shard_terms[0], shard_terms[1]), "dp")
    down_grad = summed_down * gradient_scale_factor
    scaled_up_gradient = reduced_up_gradient * (adapter_scale_factor * gradient_scale_factor)
    return (mixed_update, attention_output_gradient, down_grad, scaled_up_gradient)


MESH = pl.DeviceIdType.MESH
ORDER = (1, 3, 2)
NT = (((1,), (1,)), ((), ()))
TN = (((0,), (0,)), ((), ()))


def dot(a, b, dims=(((1,), (0,)), ((), ()))):
    return lax.dot_general(a, b, dims, preferred_element_type=jnp.float32)


class Place:
    def __init__(self):
        self.dp, self.f = lax.axis_index("dp"), lax.axis_index("fsdp")
        self.c, self.x = lax.rem(self.dp, 2), lax.rem(lax.div(self.dp, 2), 2)
        self.y, self.z = lax.rem(self.f, 2), lax.div(self.f, 2)

    def far(self, k):
        z = self.z
        if k == 1:
            return z + 1 - 2 * lax.rem(z, 2)
        if k == 2:
            return z + 2 - 4 * lax.div(z, 2)
        return 3 - z

    def device(self, way):
        if way == "c":
            return {"dp": self.dp + 1 - 2 * self.c, "fsdp": self.f}
        if way == "x":
            return {"dp": self.dp + 2 - 4 * self.x, "fsdp": self.f}
        if way == "y":
            return {"dp": self.dp, "fsdp": self.f + 1 - 2 * self.y}
        return {"dp": self.dp, "fsdp": 2 * self.far(way) + self.y}


class Post:
    def __init__(self, place, send_sems, recv_sems):
        self.place, self.ss, self.rs = place, send_sems, recv_sems
        self.index, self.sent = {}, []

    def _copy(self, name, way, src, dst):
        i = self.index.setdefault(name, len(self.index))
        return pltpu.make_async_remote_copy(
            src_ref=src,
            dst_ref=dst,
            send_sem=self.ss.at[i],
            recv_sem=self.rs.at[i],
            device_id=self.place.device(way),
            device_id_type=MESH,
        )

    def send(self, name, way, src, dst=None):
        copy = self._copy(name, way, src, src if dst is None else dst)
        copy.start()
        self.sent.append(copy)

    def wait(self, name, way, dst):
        self._copy(name, way, dst, dst).wait_recv()

    def finish(self):
        for copy in self.sent:
            copy.wait_send()


class Gather:
    def __init__(self, tag, post, place, piece):
        self.tag, self.post, self.p, self.piece = tag, post, place, piece

    def send(self, name, way, region):
        self.post.send((self.tag, name), way, region)

    def wait(self, name, way, region):
        self.post.wait((self.tag, name), way, region)

    def start(self):
        p = self.p
        own = self.piece(p.c, p.x, p.z, p.y)
        self.send("oy", "y", own)
        for k in ORDER:
            self.send(("z", k), k, own)

    def own_first(self):
        p = self.p
        got = self.piece(p.c, p.x, p.z, 1 - p.y)
        self.wait("oy", "y", got)
        self.send("ox", "x", got)
        self.send("oc1", "c", got)

    def own_second(self):
        p = self.p
        got = self.piece(p.c, 1 - p.x, p.z, 1 - p.y)
        self.wait("ox", "x", got)
        self.send("oc2", "c", got)

    def own_end(self):
        p = self.p
        self.wait("oc1", "c", self.piece(1 - p.c, p.x, p.z, 1 - p.y))
        self.wait("oc2", "c", self.piece(1 - p.c, 1 - p.x, p.z, 1 - p.y))

    def first(self, k):
        p = self.p
        got = self.piece(p.c, p.x, p.far(k), p.y)
        self.wait(("z", k), k, got)
        self.send(("x", k), "x", got)
        self.send(("y", k), "y", got)
        self.send(("c1", k), "c", got)

    def second(self, k):
        p = self.p
        zz = p.far(k)
        got = self.piece(p.c, p.x, zz, 1 - p.y)
        self.wait(("y", k), "y", got)
        self.send(("xh", k), "x", self.piece(p.c, p.x, zz, 1 - p.y, "u"))
        self.send(("c3", k), "c", got)
        got = self.piece(p.c, 1 - p.x, zz, p.y)
        self.wait(("x", k), "x", got)
        self.send(("yh", k), "y", self.piece(p.c, 1 - p.x, zz, p.y, "l"))
        self.send(("c2", k), "c", got)

    def third(self, k):
        p = self.p
        zz = p.far(k)
        for name, way, part in (("xh", "x", "u"), ("yh", "y", "l")):
            got = self.piece(p.c, 1 - p.x, zz, 1 - p.y, part)
            self.wait((name, k), way, got)
            self.send(("d" + part, k), "c", got)

    def end(self, k):
        p = self.p
        zz, c = p.far(k), 1 - p.c
        self.wait(("c1", k), "c", self.piece(c, p.x, zz, p.y))
        self.wait(("c3", k), "c", self.piece(c, p.x, zz, 1 - p.y))
        self.wait(("c2", k), "c", self.piece(c, 1 - p.x, zz, p.y))
        for part in "ul":
            self.wait(("d" + part, k), "c", self.piece(c, 1 - p.x, zz, 1 - p.y, part))


MESSAGES = 2 * (10 * len(ORDER) + 4) + 4 + 7


def kernel(
    scales,
    x_hbm, cot_hbm, codes, amax, down, up, gate, feat,
    mixed_hbm, aog_hbm, dn_out, up_out,
    w, pre, x, cot, bg, acc, mixed, aog, bacc, upf, downf, lr, bn, grow,
    gates, gf, g_send, g_got, g_sum, z_send, z_got, y_send, y_got, half, half_got, whole,
    send_sems, recv_sems, local_sems,
):
    place = Place()
    post = Post(place, send_sems, recv_sems)
    rows, width = codes.shape
    quarter = width // 4
    shard_up = up.shape[1]
    rank = up.shape[0]
    part = down.shape[0] // 3

    load_x = pltpu.make_async_copy(x_hbm, x, local_sems.at[0])
    load_x.start()
    load_cot = pltpu.make_async_copy(cot_hbm, cot, local_sems.at[1])
    load_cot.start()

    barrier = pltpu.get_barrier_semaphore()
    ways = ("c", "x", "y") + ORDER
    for way in ways:
        pl.semaphore_signal(barrier, inc=1, device_id=place.device(way), device_id_type=MESH)

    def w_piece(c, xx, zz, yy, which=""):
        start, size = {"": (0, rows), "l": (0, rows // 2), "u": (rows // 2, rows // 2)}[which]
        begin = pl.multiple_of((2 * zz + yy) * rows + start, rows // 2)
        return w.at[2 * c + xx, pl.ds(begin, size)]

    def pre_piece(c, xx, zz, yy, which=""):
        start, size = {"": (0, 48), "l": (0, 32), "u": (32, 16)}[which]
        begin = pl.multiple_of((2 * c + xx) * 48 + start, 16)
        return pre.at[2 * zz + yy, pl.ds(begin, size)]

    big = Gather("w", post, place, w_piece)
    small = Gather("p", post, place, pre_piece)
    own = pl.ds(pl.multiple_of(place.f * rows, rows), rows)
    factor = amax[...].astype(jnp.float32)

    pre[place.f, :rank, :] = up[...]
    for j in range(3):
        pre[place.f, rank:, j * 128 : (j + 1) * 128] = down[j * part : (j + 1) * part, :]
    gates[0] = dot(feat[...], gate[...])[0:1]

    def scale(q):
        columns = pl.ds(pl.multiple_of(q * quarter, 128), quarter)
        w[q, own, :] = (codes[:, columns].astype(jnp.float32) * factor).astype(jnp.bfloat16)

    mine = 2 * place.c + place.x
    scale(mine)
    pl.semaphore_wait(barrier, len(ways))

    post.send("gy", "y", gates.at[0], gates.at[1])
    small.start()
    big.start()
    for i in range(1, 4):
        scale(lax.rem(mine + i, 4))

    post.wait("gy", "y", gates.at[1])
    gates[2] = gates[0] + gates[1]
    for i, k in enumerate(ORDER):
        post.send(("gz", k), k, gates.at[2], gates.at[3 + i])
    small.own_first()
    for k in ORDER:
        small.first(k)
    small.own_second()
    for k in ORDER:
        small.second(k)
    for i, k in enumerate(ORDER):
        post.wait(("gz", k), k, gates.at[3 + i])
    grow[...] = gates[2] + gates[3] + gates[4] + gates[5]
    for k in ORDER:
        small.third(k)
    big.own_first()
    big.first(ORDER[0])
    small.own_end()
    for k in ORDER:
        small.end(k)

    @pl.loop(0, 8)
    def _(f):
        upf[:, pl.ds(pl.multiple_of(f * shard_up, 128), shard_up)] = pre[f, :rank, :]
        for j in range(3):
            to = pl.ds(pl.multiple_of(f * rows + j * part, part), part)
            downf[to, :] = pre[f, rank:, j * 128 : (j + 1) * 128]

    load_x.wait()
    load_cot.wait()
    lr[...] = dot(x[...], downf[...]).astype(jnp.bfloat16)
    bacc[:, :rank] = jnp.zeros((x.shape[0], rank), jnp.float32)

    @pl.loop(0, 4)
    def _(q):
        columns = pl.ds(pl.multiple_of(q * quarter, 128), quarter)
        branch = (cot[:, columns].astype(jnp.float32) * grow[:, columns]).astype(jnp.bfloat16)
        bg[q] = branch
        ups = upf[:, columns]
        bacc[:, :rank] += dot(branch, ups, NT)
        acc[q] = 0.5 * dot(lr[...], ups)
        term = dot(lr[...], branch, TN)
        gf[2 * q, :rank, :] = term[:, :shard_up]
        gf[2 * q + 1, :rank, :] = term[:, shard_up:]

    bn[...] = (0.5 * bacc[:, :rank]).astype(jnp.bfloat16)

    @pl.loop(0, 4)
    def _(zz):
        columns = pl.ds(pl.multiple_of(zz * 2 * rows, 128), 2 * rows)
        term = dot(x[:, columns], bn[...], TN)
        for b in range(6):
            gf[2 * zz + b // 3, rank:, (b % 3) * 128 : (b % 3 + 1) * 128] = term[b * part : (b + 1) * part]

    hrows = rows // 2
    keep = pl.ds(pl.multiple_of(place.c * hrows, hrows), hrows)
    give = pl.ds(pl.multiple_of((1 - place.c) * hrows, hrows), hrows)
    g_send[...] = gf[:, give, :].astype(jnp.bfloat16)
    post.send("rc", "c", g_send, g_got)

    big.own_second()
    big.first(ORDER[1])
    big.second(ORDER[0])

    post.wait("rc", "c", g_got)
    g_sum[...] = gf[:, keep, :] + g_got[...].astype(jnp.float32)
    z_send[...] = g_sum[...].astype(jnp.bfloat16)
    for i, k in enumerate(ORDER):
        post.send(("rz", k), k, z_send.at[pl.ds(2 * place.far(k), 2)], z_got.at[i])

    stores = []

    def plane(zz):
        at = pl.ds(pl.multiple_of(zz * 2 * rows, 128), 2 * rows)
        bacc[...] = dot(bn[...], downf[at, :], NT)

        @pl.loop(0, 4)
        def _(q):
            block = w[q, at, :]
            acc[q] += dot(x[:, at], block)
            bacc[...] += dot(bg[q], block, NT)

        aog[:, at] = bacc[...].astype(jnp.bfloat16)
        store = pltpu.make_async_copy(aog.at[:, at], aog_hbm.at[:, at], local_sems.at[2 + len(stores)])
        store.start()
        stores.append(store)

    big.own_end()
    plane(place.z)
    big.third(ORDER[0])
    big.first(ORDER[2])
    big.second(ORDER[1])

    total = g_sum[pl.ds(2 * place.z, 2)]
    for i, k in enumerate(ORDER):
        post.wait(("rz", k), k, z_got.at[i])
        total = total + z_got[i].astype(jnp.float32)
    g_sum[pl.ds(2 * place.z, 2)] = total
    y_send[...] = g_sum[2 * place.z + 1 - place.y].astype(jnp.bfloat16)
    post.send("ry", "y", y_send, y_got)

    big.end(ORDER[0])
    plane(place.far(ORDER[0]))
    big.third(ORDER[1])
    big.second(ORDER[2])

    post.wait("ry", "y", y_got)
    half[...] = g_sum[place.f] + y_got[...].astype(jnp.float32)
    post.send("rx", "x", half, half_got)

    big.end(ORDER[1])
    plane(place.far(ORDER[1]))

    post.wait("rx", "x", half_got)
    whole[place.c] = half[...] + half_got[...]
    post.send("rd", "c", whole.at[place.c])

    big.third(ORDER[2])
    post.wait("rd", "c", whole.at[1 - place.c])
    for i in range(rank // 32):
        r = i * 32
        up_out[r : r + 32, :] = whole[r // hrows, r % hrows : r % hrows + 32, :] * scales[1]
    for j in range(3):
        dn_out[j * part : (j + 1) * part, :] = (
            whole[1, rank - hrows :, j * 128 : (j + 1) * 128] * scales[0]
        )

    big.end(ORDER[2])
    plane(place.far(ORDER[2]))
    for q in range(4):
        at = pl.ds(q * quarter, quarter)
        mixed[:, at] = (acc[q] * grow[:, at]).astype(jnp.bfloat16)
        store = pltpu.make_async_copy(mixed.at[:, at], mixed_hbm.at[:, at], local_sems.at[2 + len(stores)])
        store.start()
        stores.append(store)
    post.finish()
    for store in stores:
        store.wait()


def fused(x, cot, codes, amax, down, up, gate, timesteps):
    tokens, inner = x.shape
    width, rank = cot.shape[1], up.shape[0]
    rows = codes.shape[0]
    dp_count, fsdp_count = lax.axis_size("dp"), lax.axis_size("fsdp")
    per = gate.shape[0]
    sample = (lax.axis_index("dp") * fsdp_count) * tokens // PATCHES
    step = lax.dynamic_slice_in_dim(timesteps, sample, 1).astype(jnp.float32)
    number = lax.axis_index("fsdp") * per + jnp.arange(per, dtype=jnp.int32)
    half_freq = FREQ // 2
    frequency = jnp.exp(
        -math.log(10000.0) * (number % half_freq).astype(jnp.float32) / half_freq
    )
    angle = step * frequency
    feat = jnp.where(number < half_freq, jnp.cos(angle), jnp.sin(angle)).astype(jnp.bfloat16)
    feat = jnp.broadcast_to(feat[None, :], (16, per))
    gradient_scale = (tokens * dp_count * fsdp_count) ** (-0.5)
    bf, f32 = jnp.bfloat16, jnp.float32
    quarter, hrows = width // 4, rows // 2
    vmem = pl.BlockSpec(memory_space=pltpu.VMEM)
    hbm = pl.BlockSpec(memory_space=pl.ANY)
    return pl.pallas_call(
        functools.partial(kernel, (gradient_scale, adapter_scale_factor * gradient_scale)),
        out_shape=(
            jax.ShapeDtypeStruct((tokens, width), bf),
            jax.ShapeDtypeStruct((tokens, inner), bf),
            jax.ShapeDtypeStruct((rows, rank), f32),
            jax.ShapeDtypeStruct((rank, up.shape[1]), f32),
        ),
        in_specs=[hbm, hbm] + [vmem] * 6,
        out_specs=(hbm, hbm, vmem, vmem),
        scratch_shapes=[
            pltpu.VMEM((4, inner, quarter), bf),
            pltpu.VMEM((8, rows, up.shape[1]), bf),
            pltpu.VMEM((tokens, inner), bf),
            pltpu.VMEM((tokens, width), bf),
            pltpu.VMEM((4, tokens, quarter), bf),
            pltpu.VMEM((4, tokens, quarter), f32),
            pltpu.VMEM((tokens, width), bf),
            pltpu.VMEM((tokens, inner), bf),
            pltpu.VMEM((tokens, 2 * rows), f32),
            pltpu.VMEM((rank, width), bf),
            pltpu.VMEM((inner, rank), bf),
            pltpu.VMEM((tokens, rank), bf),
            pltpu.VMEM((tokens, rank), bf),
            pltpu.VMEM((1, width), f32),
            pltpu.VMEM((6, 1, width), f32),
            pltpu.VMEM((8, rows, up.shape[1]), f32),
            pltpu.VMEM((8, hrows, up.shape[1]), bf),
            pltpu.VMEM((8, hrows, up.shape[1]), bf),
            pltpu.VMEM((8, hrows, up.shape[1]), f32),
            pltpu.VMEM((8, hrows, up.shape[1]), bf),
            pltpu.VMEM((3, 2, hrows, up.shape[1]), bf),
            pltpu.VMEM((hrows, up.shape[1]), bf),
            pltpu.VMEM((hrows, up.shape[1]), bf),
            pltpu.VMEM((hrows, up.shape[1]), f32),
            pltpu.VMEM((hrows, up.shape[1]), f32),
            pltpu.VMEM((2, hrows, up.shape[1]), f32),
            pltpu.SemaphoreType.DMA((MESSAGES,)),
            pltpu.SemaphoreType.DMA((MESSAGES,)),
            pltpu.SemaphoreType.DMA((10,)),
        ],
        compiler_params=pltpu.CompilerParams(
            collective_id=0, has_side_effects=True, vmem_limit_bytes=56 * 1024 * 1024
        ),
    )(x, cot, codes, amax[None, :], down, up, gate, feat)


def fits(mesh):
    return mesh.shape["dp"] == 4 and mesh.shape["fsdp"] == 8


def solution(mesh):
    in_specs = (
        P(("dp", "fsdp"), None),
        P(("dp", "fsdp"), None),
        P("fsdp", None),
        P("fsdp"),
        P("fsdp", None),
        P(None, "fsdp"),
        P("fsdp", None),
        P(),
    )
    out_specs = (P(("dp", "fsdp"), None), P(("dp", "fsdp"), None), P("fsdp", None), P(None, "fsdp"))
    return jax.shard_map(
        fused if fits(mesh) else per_device, mesh=mesh, in_specs=in_specs, out_specs=out_specs, check_vma=False
    )
```

```python
import functools
import math

import jax
import jax.numpy as jnp
from jax import lax
from jax.experimental import pallas as pl
from jax.experimental.pallas import tpu as pltpu
from jax.sharding import PartitionSpec as P

FREQ = 256
PATCHES = 4096


adapter_scale_factor = 0.5


def per_device(
    attention_output_rows,
    cotangent,
    quantized_weight_codes,
    shard_absolute_maximum,
    adapter_down_weight,
    adapter_up_weight,
    timestep_gate_weight,
    timesteps,
):
    row_count = attention_output_rows.shape[0]
    dp_count = lax.axis_size("dp")
    fsdp_count = lax.axis_size("fsdp")
    amax_rows = jnp.broadcast_to(shard_absolute_maximum, (quantized_weight_codes.shape[0],))
    all_codes, scales = (
        lax.all_gather(quantized_weight_codes, "fsdp", axis=0, tiled=True),
        lax.all_gather(amax_rows, "fsdp", axis=0, tiled=True),
    )
    weight = (all_codes.astype(jnp.float32) * scales.astype(jnp.float32)[:, None]).astype(
        jnp.bfloat16
    )
    down_all, gathered_up_weight, gate_all = (
        lax.all_gather(adapter_down_weight, "fsdp", axis=0, tiled=True),
        lax.all_gather(adapter_up_weight, "fsdp", axis=1, tiled=True),
        lax.all_gather(timestep_gate_weight, "fsdp", axis=0, tiled=True),
    )
    sample_index = (
        (lax.axis_index("dp") * fsdp_count + lax.axis_index("fsdp")) * row_count // PATCHES
    )
    step_value = lax.dynamic_slice_in_dim(timesteps, sample_index, 1)
    half_freq = FREQ // 2
    frequency = jnp.exp(-math.log(10000.0) * jnp.arange(half_freq, dtype=jnp.float32) / half_freq)
    phase_angle = step_value.astype(jnp.float32)[:, None] * frequency[None, :]
    features = jnp.concatenate([jnp.cos(phase_angle), jnp.sin(phase_angle)], axis=1).astype(
        jnp.bfloat16
    )
    gate_row = jnp.dot(features, gate_all, preferred_element_type=jnp.float32)
    bottleneck_activation = jnp.dot(
        attention_output_rows, down_all, preferred_element_type=jnp.float32
    ).astype(jnp.bfloat16)
    projection_output = jnp.dot(attention_output_rows, weight, preferred_element_type=jnp.float32)
    projection_output = projection_output + adapter_scale_factor * jnp.dot(
        bottleneck_activation, gathered_up_weight, preferred_element_type=jnp.float32
    )
    mixed_update = (projection_output * gate_row).astype(jnp.bfloat16)
    gated_branch_gradient = (cotangent.astype(jnp.float32) * gate_row).astype(jnp.bfloat16)
    bottleneck_gradient = (
        adapter_scale_factor
        * jnp.dot(gated_branch_gradient, gathered_up_weight.T, preferred_element_type=jnp.float32)
    ).astype(jnp.bfloat16)
    attention_output_gradient = jnp.dot(
        gated_branch_gradient, weight.T, preferred_element_type=jnp.float32
    )
    attention_output_gradient = (
        attention_output_gradient
        + jnp.dot(bottleneck_gradient, down_all.T, preferred_element_type=jnp.float32)
    ).astype(jnp.bfloat16)
    term_down = jnp.dot(
        attention_output_rows.T, bottleneck_gradient, preferred_element_type=jnp.float32
    )
    term_up = jnp.dot(
        bottleneck_activation.T, gated_branch_gradient, preferred_element_type=jnp.float32
    )
    gradient_scale_factor = (row_count * dp_count * fsdp_count) ** (-0.5)
    shard_terms = (
        lax.psum_scatter(term_down, "fsdp", scatter_dimension=0, tiled=True),
        lax.psum_scatter(term_up, "fsdp", scatter_dimension=1, tiled=True),
    )
    summed_down, reduced_up_gradient = lax.psum((shard_terms[0], shard_terms[1]), "dp")
    down_grad = summed_down * gradient_scale_factor
    scaled_up_gradient = reduced_up_gradient * (adapter_scale_factor * gradient_scale_factor)
    return (mixed_update, attention_output_gradient, down_grad, scaled_up_gradient)


MESH = pl.DeviceIdType.MESH
ORDER = (1, 3, 2)
NT = (((1,), (1,)), ((), ()))
TN = (((0,), (0,)), ((), ()))


def dot(a, b, dims=(((1,), (0,)), ((), ()))):
    return lax.dot_general(a, b, dims, preferred_element_type=jnp.float32)


class Place:
    def __init__(self):
        self.dp, self.f = lax.axis_index("dp"), lax.axis_index("fsdp")
        self.c, self.x = lax.rem(self.dp, 2), lax.rem(lax.div(self.dp, 2), 2)
        self.y, self.z = lax.rem(self.f, 2), lax.div(self.f, 2)

    def far(self, k):
        z = self.z
        if k == 1:
            return z + 1 - 2 * lax.rem(z, 2)
        if k == 2:
            return z + 2 - 4 * lax.div(z, 2)
        return 3 - z

    def device(self, way):
        if way == "c":
            return {"dp": self.dp + 1 - 2 * self.c, "fsdp": self.f}
        if way == "x":
            return {"dp": self.dp + 2 - 4 * self.x, "fsdp": self.f}
        if way == "y":
            return {"dp": self.dp, "fsdp": self.f + 1 - 2 * self.y}
        return {"dp": self.dp, "fsdp": 2 * self.far(way) + self.y}


class Post:
    def __init__(self, place, send_sems, recv_sems):
        self.place, self.ss, self.rs = place, send_sems, recv_sems
        self.index, self.sent = {}, []

    def _copy(self, name, way, src, dst):
        i = self.index.setdefault(name, len(self.index))
        return pltpu.make_async_remote_copy(
            src_ref=src,
            dst_ref=dst,
            send_sem=self.ss.at[i],
            recv_sem=self.rs.at[i],
            device_id=self.place.device(way),
            device_id_type=MESH,
        )

    def send(self, name, way, src, dst=None):
        copy = self._copy(name, way, src, src if dst is None else dst)
        copy.start()
        self.sent.append(copy)

    def wait(self, name, way, dst):
        self._copy(name, way, dst, dst).wait_recv()

    def finish(self):
        for copy in self.sent:
            copy.wait_send()


class Gather:
    def __init__(self, tag, post, place, piece):
        self.tag, self.post, self.p, self.piece = tag, post, place, piece

    def send(self, name, way, region):
        self.post.send((self.tag, name), way, region)

    def wait(self, name, way, region):
        self.post.wait((self.tag, name), way, region)

    def start_own(self):
        p = self.p
        for h in "lu":
            self.send(("oy", h), "y", self.piece(p.c, p.x, p.z, p.y, h))

    def start(self, k):
        p = self.p
        for h in "lu":
            self.send(("z", k, h), k, self.piece(p.c, p.x, p.z, p.y, h))

    def own_first(self, h):
        p = self.p
        got = self.piece(p.c, p.x, p.z, 1 - p.y, h)
        self.wait(("oy", h), "y", got)
        self.send(("ox", h), "x", got)
        self.send(("oc1", h), "c", got)

    def own_second(self, h):
        p = self.p
        got = self.piece(p.c, 1 - p.x, p.z, 1 - p.y, h)
        self.wait(("ox", h), "x", got)
        self.send(("oc2", h), "c", got)

    def own_end(self, same):
        p = self.p
        for h in "lu":
            if same:
                self.wait(("oc1", h), "c", self.piece(1 - p.c, p.x, p.z, 1 - p.y, h))
            else:
                self.wait(("oc2", h), "c", self.piece(1 - p.c, 1 - p.x, p.z, 1 - p.y, h))

    def first(self, k, h):
        p = self.p
        got = self.piece(p.c, p.x, p.far(k), p.y, h)
        self.wait(("z", k, h), k, got)
        self.send(("x", k, h), "x", got)
        self.send(("y", k, h), "y", got)
        self.send(("c1", k, h), "c", got)

    def second(self, k, h):
        p = self.p
        zz = p.far(k)
        got = self.piece(p.c, p.x, zz, 1 - p.y, h)
        self.wait(("y", k, h), "y", got)
        if h == "u":
            self.send(("d", k, h), "x", got)
        self.send(("c3", k, h), "c", got)
        got = self.piece(p.c, 1 - p.x, zz, p.y, h)
        self.wait(("x", k, h), "x", got)
        if h == "l":
            self.send(("d", k, h), "y", got)
        self.send(("c2", k, h), "c", got)

    def third(self, k):
        p = self.p
        for h in "lu":
            got = self.piece(p.c, 1 - p.x, p.far(k), 1 - p.y, h)
            self.wait(("d", k, h), "y" if h == "l" else "x", got)
            self.send(("c4", k, h), "c", got)

    def end(self, k, same):
        p = self.p
        zz, c = p.far(k), 1 - p.c
        for h in "lu":
            if same:
                self.wait(("c1", k, h), "c", self.piece(c, p.x, zz, p.y, h))
                self.wait(("c3", k, h), "c", self.piece(c, p.x, zz, 1 - p.y, h))
            else:
                self.wait(("c2", k, h), "c", self.piece(c, 1 - p.x, zz, p.y, h))
                self.wait(("c4", k, h), "c", self.piece(c, 1 - p.x, zz, 1 - p.y, h))


MESSAGES = 2 * (16 * len(ORDER) + 8) + 4 + 7


def kernel(
    scales,
    x_hbm, cot_hbm, codes, amax, down, up, gate, feat,
    mixed_hbm, aog_hbm, dn_out, up_out,
    w, pre, x, cot, bg, acc, mixed, aog, bacc, bsum, upf, downf, lr, bn, grow,
    gates, gf, g_send, g_got, g_sum, z_send, z_got, y_send, y_got, half, half_got, whole,
    send_sems, recv_sems, local_sems,
):
    place = Place()
    post = Post(place, send_sems, recv_sems)
    rows, width = codes.shape
    quarter = width // 4
    shard_up = up.shape[1]
    rank = up.shape[0]
    part = down.shape[0] // 3

    load_x = pltpu.make_async_copy(x_hbm, x, local_sems.at[0])
    load_x.start()
    load_cot = pltpu.make_async_copy(cot_hbm, cot, local_sems.at[1])
    load_cot.start()

    barrier = pltpu.get_barrier_semaphore()
    ways = ("c", "x", "y") + ORDER
    for way in ways:
        pl.semaphore_signal(barrier, inc=1, device_id=place.device(way), device_id_type=MESH)

    def w_piece(c, xx, zz, yy, which):
        start, size = {"l": (0, rows // 2), "u": (rows // 2, rows // 2)}[which]
        begin = pl.multiple_of((2 * zz + yy) * rows + start, rows // 2)
        return w.at[2 * c + xx, pl.ds(begin, size)]

    def pre_piece(c, xx, zz, yy, which):
        start, size = {"l": (0, 32), "u": (32, 16)}[which]
        begin = pl.multiple_of((2 * c + xx) * 48 + start, 16)
        return pre.at[2 * zz + yy, pl.ds(begin, size)]

    big = Gather("w", post, place, w_piece)
    small = Gather("p", post, place, pre_piece)
    own = pl.ds(pl.multiple_of(place.f * rows, rows), rows)
    factor = amax[...].astype(jnp.float32)

    pre[place.f, :rank, :] = up[...]
    for j in range(3):
        pre[place.f, rank:, j * 128 : (j + 1) * 128] = down[j * part : (j + 1) * part, :]
    gates[0] = dot(feat[...], gate[...])[0:1]

    def scale(q):
        columns = pl.ds(pl.multiple_of(q * quarter, 128), quarter)
        w[q, own, :] = (codes[:, columns].astype(jnp.float32) * factor).astype(jnp.bfloat16)

    mine = 2 * place.c + place.x
    scale(mine)
    pl.semaphore_wait(barrier, len(ways))

    post.send("gy", "y", gates.at[0], gates.at[1])
    small.start_own()
    for k in ORDER:
        small.start(k)
    big.start(1)
    big.start_own()
    big.start(3)
    for i in range(1, 4):
        scale(lax.rem(mine + i, 4))

    post.wait("gy", "y", gates.at[1])
    gates[2] = gates[0] + gates[1]
    for i, k in enumerate(ORDER):
        post.send(("gz", k), k, gates.at[2], gates.at[3 + i])
    for h in "lu":
        small.own_first(h)
    for k in ORDER:
        for h in "lu":
            small.first(k, h)
    big.own_first("l")
    for h in "lu":
        small.own_second(h)
    for k in ORDER:
        for h in "lu":
            small.second(k, h)
    big.own_first("u")
    for k in ORDER:
        small.third(k)
    for i, k in enumerate(ORDER):
        post.wait(("gz", k), k, gates.at[3 + i])
    grow[...] = gates[2] + gates[3] + gates[4] + gates[5]
    for same in (True, False):
        small.own_end(same)
        for k in ORDER:
            small.end(k, same)

    @pl.loop(0, 8)
    def _(f):
        upf[:, pl.ds(pl.multiple_of(f * shard_up, 128), shard_up)] = pre[f, :rank, :]
        for j in range(3):
            to = pl.ds(pl.multiple_of(f * rows + j * part, part), part)
            downf[to, :] = pre[f, rank:, j * 128 : (j + 1) * 128]

    load_x.wait()
    load_cot.wait()
    big.first(1, "l")
    lr[...] = dot(x[...], downf[...]).astype(jnp.bfloat16)
    bsum[...] = jnp.zeros_like(bsum)
    big.first(1, "u")
    big.start(2)

    def adapter(begin, end):
        @pl.loop(begin, end)
        def _(q):
            columns = pl.ds(pl.multiple_of(q * quarter, 128), quarter)
            branch = (cot[:, columns].astype(jnp.float32) * grow[:, columns]).astype(jnp.bfloat16)
            bg[q] = branch
            ups = upf[:, columns]
            bsum[...] += dot(branch, ups, NT)
            acc[q] = 0.5 * dot(lr[...], ups)
            term = dot(lr[...], branch, TN)
            gf[2 * q, :rank, :] = term[:, :shard_up]
            gf[2 * q + 1, :rank, :] = term[:, shard_up:]

    adapter(0, 2)
    big.own_second("l")
    big.own_second("u")
    adapter(2, 4)
    big.second(1, "l")
    bn[...] = (0.5 * bsum[...]).astype(jnp.bfloat16)

    @pl.loop(0, 4)
    def _(zz):
        columns = pl.ds(pl.multiple_of(zz * 2 * rows, 128), 2 * rows)
        term = dot(x[:, columns], bn[...], TN)
        for b in range(6):
            gf[2 * zz + b // 3, rank:, (b % 3) * 128 : (b % 3 + 1) * 128] = term[b * part : (b + 1) * part]

    hrows = rows // 2
    keep = pl.ds(pl.multiple_of(place.c * hrows, hrows), hrows)
    give = pl.ds(pl.multiple_of((1 - place.c) * hrows, hrows), hrows)
    g_send[...] = gf[:, give, :].astype(jnp.bfloat16)
    post.send("rc", "c", g_send, g_got)

    stores = []

    def keep_store(source, target):
        store = pltpu.make_async_copy(source, target, local_sems.at[2 + len(stores)])
        store.start()
        stores.append(store)

    done = [0, 0, 0, 0]
    quarters = {
        "a": 2 * place.c + place.x,
        "b": 2 * place.c + 1 - place.x,
        "d": 2 - 2 * place.c + place.x,
        "e": 2 - 2 * place.c + 1 - place.x,
    }

    def unit(k, which, last=False):
        zz = place.far(k) if k else place.z
        q = quarters[which]
        at = pl.ds(pl.multiple_of(zz * 2 * rows, 128), 2 * rows)
        block = w[q, at, :]
        back = dot(bg[q], block, NT)
        if done[k] == 0:
            bacc[k] = back + dot(bn[...], downf[at, :], NT)
        elif done[k] < 3:
            bacc[k] += back
        else:
            aog[:, at] = (bacc[k] + back).astype(jnp.bfloat16)
            keep_store(aog.at[:, at], aog_hbm.at[:, at])
        done[k] += 1
        total = acc[q] + dot(x[:, at], block)
        if last:
            columns = pl.ds(pl.multiple_of(q * quarter, 128), quarter)
            mixed[:, columns] = (total * grow[:, columns]).astype(jnp.bfloat16)
            keep_store(mixed.at[:, columns], mixed_hbm.at[:, columns])
        else:
            acc[q] = total

    big.first(3, "l")
    big.first(3, "u")
    big.second(1, "u")
    unit(0, "a")
    unit(0, "b")
    big.third(1)

    post.wait("rc", "c", g_got)
    g_sum[...] = gf[:, keep, :] + g_got[...].astype(jnp.float32)
    z_send[...] = g_sum[...].astype(jnp.bfloat16)
    for i, k in enumerate(ORDER):
        post.send(("rz", k), k, z_send.at[pl.ds(2 * place.far(k), 2)], z_got.at[i])

    big.first(2, "l")
    big.second(3, "l")
    big.first(2, "u")
    big.second(3, "u")
    big.own_end(True)
    unit(0, "d")
    big.own_end(False)
    unit(0, "e")
    big.third(3)
    unit(1, "a")
    big.second(2, "l")
    unit(1, "b")

    total = g_sum[pl.ds(2 * place.z, 2)]
    for i, k in enumerate(ORDER):
        post.wait(("rz", k), k, z_got.at[i])
        total = total + z_got[i].astype(jnp.float32)
    g_sum[pl.ds(2 * place.z, 2)] = total
    y_send[...] = g_sum[2 * place.z + 1 - place.y].astype(jnp.bfloat16)
    post.send("ry", "y", y_send, y_got)

    big.second(2, "u")
    big.end(1, True)
    unit(1, "d")
    big.end(1, False)
    unit(1, "e")
    unit(3, "a")
    post.wait("ry", "y", y_got)
    half[...] = g_sum[place.f] + y_got[...].astype(jnp.float32)
    post.send("rx", "x", half, half_got)
    unit(3, "b")
    big.third(2)
    unit(2, "a", True)
    big.end(3, True)
    unit(3, "d")
    big.end(3, False)
    unit(3, "e")

    post.wait("rx", "x", half_got)
    whole[place.c] = half[...] + half_got[...]
    post.send("rd", "c", whole.at[place.c])
    big.end(2, True)
    unit(2, "d", True)
    unit(2, "b", True)
    post.wait("rd", "c", whole.at[1 - place.c])
    for i in range(rank // 32):
        r = i * 32
        up_out[r : r + 32, :] = whole[r // hrows, r % hrows : r % hrows + 32, :] * scales[1]
    for j in range(3):
        dn_out[j * part : (j + 1) * part, :] = (
            whole[1, rank - hrows :, j * 128 : (j + 1) * 128] * scales[0]
        )
    big.end(2, False)
    unit(2, "e", True)
    post.finish()
    for store in stores:
        store.wait()


def fused(x, cot, codes, amax, down, up, gate, timesteps):
    tokens, inner = x.shape
    width, rank = cot.shape[1], up.shape[0]
    rows = codes.shape[0]
    dp_count, fsdp_count = lax.axis_size("dp"), lax.axis_size("fsdp")
    per = gate.shape[0]
    sample = (lax.axis_index("dp") * fsdp_count) * tokens // PATCHES
    chosen = jnp.arange(timesteps.shape[0], dtype=jnp.int32) == sample
    step = jnp.sum(jnp.where(chosen, timesteps, 0)).astype(jnp.float32)
    number = lax.axis_index("fsdp") * per + jnp.arange(per, dtype=jnp.int32)
    half_freq = FREQ // 2
    frequency = jnp.exp(
        -math.log(10000.0) * (number % half_freq).astype(jnp.float32) / half_freq
    )
    angle = step * frequency
    feat = jnp.where(number < half_freq, jnp.cos(angle), jnp.sin(angle)).astype(jnp.bfloat16)
    feat = jnp.broadcast_to(feat[None, :], (16, per))
    gradient_scale = (tokens * dp_count * fsdp_count) ** (-0.5)
    bf, f32 = jnp.bfloat16, jnp.float32
    quarter, hrows = width // 4, rows // 2
    vmem = pl.BlockSpec(memory_space=pltpu.VMEM)
    hbm = pl.BlockSpec(memory_space=pl.ANY)
    return pl.pallas_call(
        functools.partial(kernel, (gradient_scale, adapter_scale_factor * gradient_scale)),
        out_shape=(
            jax.ShapeDtypeStruct((tokens, width), bf),
            jax.ShapeDtypeStruct((tokens, inner), bf),
            jax.ShapeDtypeStruct((rows, rank), f32),
            jax.ShapeDtypeStruct((rank, up.shape[1]), f32),
        ),
        in_specs=[hbm, hbm] + [vmem] * 6,
        out_specs=(hbm, hbm, vmem, vmem),
        scratch_shapes=[
            pltpu.VMEM((4, inner, quarter), bf),
            pltpu.VMEM((8, rows, up.shape[1]), bf),
            pltpu.VMEM((tokens, inner), bf),
            pltpu.VMEM((tokens, width), bf),
            pltpu.VMEM((4, tokens, quarter), bf),
            pltpu.VMEM((4, tokens, quarter), f32),
            pltpu.VMEM((tokens, width), bf),
            pltpu.VMEM((tokens, inner), bf),
            pltpu.VMEM((4, tokens, 2 * rows), f32),
            pltpu.VMEM((tokens, rank), f32),
            pltpu.VMEM((rank, width), bf),
            pltpu.VMEM((inner, rank), bf),
            pltpu.VMEM((tokens, rank), bf),
            pltpu.VMEM((tokens, rank), bf),
            pltpu.VMEM((1, width), f32),
            pltpu.VMEM((6, 1, width), f32),
            pltpu.VMEM((8, rows, up.shape[1]), f32),
            pltpu.VMEM((8, hrows, up.shape[1]), bf),
            pltpu.VMEM((8, hrows, up.shape[1]), bf),
            pltpu.VMEM((8, hrows, up.shape[1]), f32),
            pltpu.VMEM((8, hrows, up.shape[1]), bf),
            pltpu.VMEM((3, 2, hrows, up.shape[1]), bf),
            pltpu.VMEM((hrows, up.shape[1]), bf),
            pltpu.VMEM((hrows, up.shape[1]), bf),
            pltpu.VMEM((hrows, up.shape[1]), f32),
            pltpu.VMEM((hrows, up.shape[1]), f32),
            pltpu.VMEM((2, hrows, up.shape[1]), f32),
            pltpu.SemaphoreType.DMA((MESSAGES,)),
            pltpu.SemaphoreType.DMA((MESSAGES,)),
            pltpu.SemaphoreType.DMA((10,)),
        ],
        compiler_params=pltpu.CompilerParams(
            collective_id=0, has_side_effects=True, vmem_limit_bytes=56 * 1024 * 1024
        ),
    )(x, cot, codes, amax[None, :], down, up, gate, feat)


def fits(mesh):
    return mesh.shape["dp"] == 4 and mesh.shape["fsdp"] == 8


def solution(mesh):
    in_specs = (
        P(("dp", "fsdp"), None),
        P(("dp", "fsdp"), None),
        P("fsdp", None),
        P("fsdp"),
        P("fsdp", None),
        P(None, "fsdp"),
        P("fsdp", None),
        P(),
    )
    out_specs = (P(("dp", "fsdp"), None), P(("dp", "fsdp"), None), P("fsdp", None), P(None, "fsdp"))
    return jax.shard_map(
        fused if fits(mesh) else per_device, mesh=mesh, in_specs=in_specs, out_specs=out_specs, check_vma=False
    )
```

```python
import functools
import math

import jax
import jax.numpy as jnp
from jax import lax
from jax.experimental import pallas as pl
from jax.experimental.pallas import tpu as pltpu
from jax.sharding import PartitionSpec as P

FREQ = 256
PATCHES = 4096


adapter_scale_factor = 0.5


def per_device(
    attention_output_rows,
    cotangent,
    quantized_weight_codes,
    shard_absolute_maximum,
    adapter_down_weight,
    adapter_up_weight,
    timestep_gate_weight,
    timesteps,
):
    row_count = attention_output_rows.shape[0]
    dp_count = lax.axis_size("dp")
    fsdp_count = lax.axis_size("fsdp")
    amax_rows = jnp.broadcast_to(shard_absolute_maximum, (quantized_weight_codes.shape[0],))
    all_codes, scales = (
        lax.all_gather(quantized_weight_codes, "fsdp", axis=0, tiled=True),
        lax.all_gather(amax_rows, "fsdp", axis=0, tiled=True),
    )
    weight = (all_codes.astype(jnp.float32) * scales.astype(jnp.float32)[:, None]).astype(
        jnp.bfloat16
    )
    down_all, gathered_up_weight, gate_all = (
        lax.all_gather(adapter_down_weight, "fsdp", axis=0, tiled=True),
        lax.all_gather(adapter_up_weight, "fsdp", axis=1, tiled=True),
        lax.all_gather(timestep_gate_weight, "fsdp", axis=0, tiled=True),
    )
    sample_index = (
        (lax.axis_index("dp") * fsdp_count + lax.axis_index("fsdp")) * row_count // PATCHES
    )
    step_value = lax.dynamic_slice_in_dim(timesteps, sample_index, 1)
    half_freq = FREQ // 2
    frequency = jnp.exp(-math.log(10000.0) * jnp.arange(half_freq, dtype=jnp.float32) / half_freq)
    phase_angle = step_value.astype(jnp.float32)[:, None] * frequency[None, :]
    features = jnp.concatenate([jnp.cos(phase_angle), jnp.sin(phase_angle)], axis=1).astype(
        jnp.bfloat16
    )
    gate_row = jnp.dot(features, gate_all, preferred_element_type=jnp.float32)
    bottleneck_activation = jnp.dot(
        attention_output_rows, down_all, preferred_element_type=jnp.float32
    ).astype(jnp.bfloat16)
    projection_output = jnp.dot(attention_output_rows, weight, preferred_element_type=jnp.float32)
    projection_output = projection_output + adapter_scale_factor * jnp.dot(
        bottleneck_activation, gathered_up_weight, preferred_element_type=jnp.float32
    )
    mixed_update = (projection_output * gate_row).astype(jnp.bfloat16)
    gated_branch_gradient = (cotangent.astype(jnp.float32) * gate_row).astype(jnp.bfloat16)
    bottleneck_gradient = (
        adapter_scale_factor
        * jnp.dot(gated_branch_gradient, gathered_up_weight.T, preferred_element_type=jnp.float32)
    ).astype(jnp.bfloat16)
    attention_output_gradient = jnp.dot(
        gated_branch_gradient, weight.T, preferred_element_type=jnp.float32
    )
    attention_output_gradient = (
        attention_output_gradient
        + jnp.dot(bottleneck_gradient, down_all.T, preferred_element_type=jnp.float32)
    ).astype(jnp.bfloat16)
    term_down = jnp.dot(
        attention_output_rows.T, bottleneck_gradient, preferred_element_type=jnp.float32
    )
    term_up = jnp.dot(
        bottleneck_activation.T, gated_branch_gradient, preferred_element_type=jnp.float32
    )
    gradient_scale_factor = (row_count * dp_count * fsdp_count) ** (-0.5)
    shard_terms = (
        lax.psum_scatter(term_down, "fsdp", scatter_dimension=0, tiled=True),
        lax.psum_scatter(term_up, "fsdp", scatter_dimension=1, tiled=True),
    )
    summed_down, reduced_up_gradient = lax.psum((shard_terms[0], shard_terms[1]), "dp")
    down_grad = summed_down * gradient_scale_factor
    scaled_up_gradient = reduced_up_gradient * (adapter_scale_factor * gradient_scale_factor)
    return (mixed_update, attention_output_gradient, down_grad, scaled_up_gradient)


MESH = pl.DeviceIdType.MESH
ORDER = (1, 3, 2)
NT = (((1,), (1,)), ((), ()))
TN = (((0,), (0,)), ((), ()))


def dot(a, b, dims=(((1,), (0,)), ((), ()))):
    return lax.dot_general(a, b, dims, preferred_element_type=jnp.float32)


class Place:
    def __init__(self):
        self.dp, self.f = lax.axis_index("dp"), lax.axis_index("fsdp")
        self.c, self.x = lax.rem(self.dp, 2), lax.rem(lax.div(self.dp, 2), 2)
        self.y, self.z = lax.rem(self.f, 2), lax.div(self.f, 2)
        self.inner = lax.rem(self.z + 1, 4) > 1

    def far(self, k):
        z = self.z
        if k == 1:
            return z + 1 - 2 * lax.rem(z, 2)
        if k == 2:
            return z + 2 - 4 * lax.div(z, 2)
        return 3 - z

    def plane(self, k):
        upper = lax.div(self.z, 2)
        if k == 1:
            return self.far(1)
        return 2 - upper if k == 2 else 3 - 3 * upper

    def device(self, way):
        if way == "c":
            return {"dp": self.dp + 1 - 2 * self.c, "fsdp": self.f}
        if way == "x":
            return {"dp": self.dp + 2 - 4 * self.x, "fsdp": self.f}
        if way == "y":
            return {"dp": self.dp, "fsdp": self.f + 1 - 2 * self.y}
        return {"dp": self.dp, "fsdp": 2 * self.far(way) + self.y}


class Post:
    def __init__(self, place, send_sems, recv_sems):
        self.place, self.ss, self.rs = place, send_sems, recv_sems
        self.index, self.sent, self.sent_inner = {}, [], []

    def _copy(self, name, way, src, dst, sender=None):
        i = self.index.setdefault(name, len(self.index))
        j = self.index.setdefault(sender or name, len(self.index))
        return pltpu.make_async_remote_copy(
            src_ref=src,
            dst_ref=dst,
            send_sem=self.ss.at[j],
            recv_sem=self.rs.at[i],
            device_id=self.place.device(way),
            device_id_type=MESH,
        )

    def send(self, name, way, src, dst=None):
        copy = self._copy(name, way, src, src if dst is None else dst)
        copy.start()
        self.sent.append(copy)

    def send_inner(self, name, way, src, sender):
        copy = self._copy(name, way, src, src, sender)
        pl.when(self.place.inner)(copy.start)
        self.sent_inner.append(copy)

    def wait(self, name, way, dst):
        self._copy(name, way, dst, dst).wait_recv()

    def finish(self):
        for copy in self.sent:
            copy.wait_send()

        @pl.when(self.place.inner)
        def _():
            for copy in self.sent_inner:
                copy.wait_send()


class Gather:
    def __init__(self, tag, post, place, piece, chain):
        self.tag, self.post, self.p, self.piece = tag, post, place, piece
        self.chain, self.far = chain, place.plane if chain else place.far

    def send(self, name, way, region):
        self.post.send((self.tag, name), way, region)

    def wait(self, name, way, region):
        self.post.wait((self.tag, name), way, region)

    def start_own(self):
        p = self.p
        for h in "lu":
            self.send(("oy", h), "y", self.piece(p.c, p.x, p.z, p.y, h))

    def start(self, k):
        p = self.p
        for h in "lu":
            own = self.piece(p.c, p.x, p.z, p.y, h)
            if self.chain and k == 3:
                self.relay(2, k, own, h, "own")
            else:
                self.send(("z", k, h), k, own)

    def relay(self, k, way, region, h, why):
        self.post.send_inner((self.tag, ("z", k, h)), way, region, (self.tag, why, k, h))

    def own_first(self, h):
        p = self.p
        got = self.piece(p.c, p.x, p.z, 1 - p.y, h)
        self.wait(("oy", h), "y", got)
        self.send(("ox", h), "x", got)
        self.send(("oc1", h), "c", got)

    def own_second(self, h):
        p = self.p
        got = self.piece(p.c, 1 - p.x, p.z, 1 - p.y, h)
        self.wait(("ox", h), "x", got)
        self.send(("oc2", h), "c", got)

    def own_end(self, same):
        p = self.p
        for h in "lu":
            if same:
                self.wait(("oc1", h), "c", self.piece(1 - p.c, p.x, p.z, 1 - p.y, h))
            else:
                self.wait(("oc2", h), "c", self.piece(1 - p.c, 1 - p.x, p.z, 1 - p.y, h))

    def first(self, k, h):
        p = self.p
        got = self.piece(p.c, p.x, self.far(k), p.y, h)
        self.wait(("z", k, h), k, got)
        if self.chain:
            if k == 1:
                self.relay(3, 3, got, h, "across")
            else:
                self.relay(k, 1, got, h, "out")
        self.send(("x", k, h), "x", got)
        self.send(("y", k, h), "y", got)
        self.send(("c1", k, h), "c", got)

    def second(self, k, h):
        p = self.p
        zz = self.far(k)
        got = self.piece(p.c, p.x, zz, 1 - p.y, h)
        self.wait(("y", k, h), "y", got)
        if h == "u":
            self.send(("d", k, h), "x", got)
        self.send(("c3", k, h), "c", got)
        got = self.piece(p.c, 1 - p.x, zz, p.y, h)
        self.wait(("x", k, h), "x", got)
        if h == "l":
            self.send(("d", k, h), "y", got)
        self.send(("c2", k, h), "c", got)

    def third(self, k):
        p = self.p
        for h in "lu":
            got = self.piece(p.c, 1 - p.x, self.far(k), 1 - p.y, h)
            self.wait(("d", k, h), "y" if h == "l" else "x", got)
            self.send(("c4", k, h), "c", got)

    def end(self, k, same):
        p = self.p
        zz, c = self.far(k), 1 - p.c
        for h in "lu":
            if same:
                self.wait(("c1", k, h), "c", self.piece(c, p.x, zz, p.y, h))
                self.wait(("c3", k, h), "c", self.piece(c, p.x, zz, 1 - p.y, h))
            else:
                self.wait(("c2", k, h), "c", self.piece(c, 1 - p.x, zz, p.y, h))
                self.wait(("c4", k, h), "c", self.piece(c, 1 - p.x, zz, 1 - p.y, h))


MESSAGES = 2 * (16 * len(ORDER) + 8) + 4 + 7 + 8


def kernel(
    scales, samples,
    x_hbm, cot_hbm, codes, down, up, gate, feat,
    mixed_hbm, aog_hbm, dn_out, up_out,
    w, pre, x, cot, bg, acc, mixed, aog, bacc, bsum, upf, downf, lr, bn, grow,
    partial, gates, gf, g_send, g_got, g_sum, z_send, z_got, y_send, y_got, half, half_got, whole,
    send_sems, recv_sems, local_sems,
):
    place = Place()
    post = Post(place, send_sems, recv_sems)
    rows, width = codes.shape
    quarter = width // 4
    shard_up = up.shape[1]
    rank = up.shape[0]
    part = down.shape[0] // 3

    load_x = pltpu.make_async_copy(x_hbm, x, local_sems.at[0])
    load_x.start()
    load_cot = pltpu.make_async_copy(cot_hbm, cot, local_sems.at[1])
    load_cot.start()

    barrier = pltpu.get_barrier_semaphore()
    ways = ("c", "x", "y") + ORDER
    for way in ways:
        pl.semaphore_signal(barrier, inc=1, device_id=place.device(way), device_id_type=MESH)

    def w_piece(c, xx, zz, yy, which):
        start, size = {"l": (0, rows // 2), "u": (rows // 2, rows // 2)}[which]
        begin = pl.multiple_of((2 * zz + yy) * rows + start, rows // 2)
        return w.at[2 * c + xx, pl.ds(begin, size)]

    def pre_piece(c, xx, zz, yy, which):
        start, size = {"l": (0, 32), "u": (32, 16)}[which]
        begin = pl.multiple_of((2 * c + xx) * 48 + start, 16)
        return pre.at[2 * zz + yy, pl.ds(begin, size)]

    big = Gather("w", post, place, w_piece, True)
    small = Gather("p", post, place, pre_piece, False)
    own = pl.ds(pl.multiple_of(place.f * rows, rows), rows)
    per = gate.shape[0]
    factor = feat[0:1, per : per + 1]

    pre[place.f, :rank, :] = up[...]
    for j in range(3):
        pre[place.f, rank:, j * 128 : (j + 1) * 128] = down[j * part : (j + 1) * part, :]
    partial[...] = dot(feat[:, :per].astype(jnp.bfloat16), gate[...])
    sample = lax.div(place.dp * samples[0], samples[1])
    gates[0] = partial[pl.ds(sample, 1), :]

    def scale(q):
        columns = pl.ds(pl.multiple_of(q * quarter, 128), quarter)
        w[q, own, :] = (codes[:, columns].astype(jnp.float32) * factor).astype(jnp.bfloat16)

    mine = 2 * place.c + place.x
    scale(mine)
    pl.semaphore_wait(barrier, len(ways))

    post.send("gy", "y", gates.at[0], gates.at[1])
    small.start_own()
    for k in ORDER:
        small.start(k)
    big.start(1)
    big.start_own()
    big.start(3)
    for i in range(1, 4):
        scale(lax.rem(mine + i, 4))

    post.wait("gy", "y", gates.at[1])
    gates[2] = gates[0] + gates[1]
    for i, k in enumerate(ORDER):
        post.send(("gz", k), k, gates.at[2], gates.at[3 + i])
    for h in "lu":
        small.own_first(h)
    for k in ORDER:
        for h in "lu":
            small.first(k, h)
    big.own_first("l")
    for h in "lu":
        small.own_second(h)
    for k in ORDER:
        for h in "lu":
            small.second(k, h)
    big.first(1, "l")
    big.own_first("u")
    for k in ORDER:
        small.third(k)
    big.first(1, "u")
    for i, k in enumerate(ORDER):
        post.wait(("gz", k), k, gates.at[3 + i])
    grow[...] = gates[2] + gates[3] + gates[4] + gates[5]
    for same in (True, False):
        small.own_end(same)
        for k in ORDER:
            small.end(k, same)

    @pl.loop(0, 8)
    def _(f):
        upf[:, pl.ds(pl.multiple_of(f * shard_up, 128), shard_up)] = pre[f, :rank, :]
        for j in range(3):
            to = pl.ds(pl.multiple_of(f * rows + j * part, part), part)
            downf[to, :] = pre[f, rank:, j * 128 : (j + 1) * 128]

    load_x.wait()
    load_cot.wait()
    lr[...] = dot(x[...], downf[...]).astype(jnp.bfloat16)
    bsum[...] = jnp.zeros_like(bsum)
    big.own_second("l")

    def adapter(begin, end):
        @pl.loop(begin, end)
        def _(q):
            columns = pl.ds(pl.multiple_of(q * quarter, 128), quarter)
            branch = (cot[:, columns].astype(jnp.float32) * grow[:, columns]).astype(jnp.bfloat16)
            bg[q] = branch
            ups = upf[:, columns]
            bsum[...] += dot(branch, ups, NT)
            acc[q] = 0.5 * dot(lr[...], ups)
            term = dot(lr[...], branch, TN)
            gf[2 * q, :rank, :] = term[:, :shard_up]
            gf[2 * q + 1, :rank, :] = term[:, shard_up:]

    adapter(0, 2)
    big.first(2, "l")
    big.first(2, "u")
    big.own_second("u")
    big.second(1, "l")
    adapter(2, 4)
    big.second(1, "u")
    bn[...] = (0.5 * bsum[...]).astype(jnp.bfloat16)

    @pl.loop(0, 4)
    def _(zz):
        columns = pl.ds(pl.multiple_of(zz * 2 * rows, 128), 2 * rows)
        term = dot(x[:, columns], bn[...], TN)
        for b in range(6):
            gf[2 * zz + b // 3, rank:, (b % 3) * 128 : (b % 3 + 1) * 128] = term[b * part : (b + 1) * part]

    hrows = rows // 2
    keep = pl.ds(pl.multiple_of(place.c * hrows, hrows), hrows)
    give = pl.ds(pl.multiple_of((1 - place.c) * hrows, hrows), hrows)
    g_send[...] = gf[:, give, :].astype(jnp.bfloat16)
    post.send("rc", "c", g_send, g_got)

    stores = []

    def keep_store(source, target):
        store = pltpu.make_async_copy(source, target, local_sems.at[2 + len(stores)])
        store.start()
        stores.append(store)

    done = [0, 0, 0, 0]
    quarters = {
        "a": 2 * place.c + place.x,
        "b": 2 * place.c + 1 - place.x,
        "d": 2 - 2 * place.c + place.x,
        "e": 2 - 2 * place.c + 1 - place.x,
    }

    def unit(k, which, last=False):
        zz = place.plane(k) if k else place.z
        q = quarters[which]
        at = pl.ds(pl.multiple_of(zz * 2 * rows, 128), 2 * rows)
        block = w[q, at, :]
        back = dot(bg[q], block, NT)
        if done[k] == 0:
            bacc[k] = back + dot(bn[...], downf[at, :], NT)
        elif done[k] < 3:
            bacc[k] += back
        else:
            aog[:, at] = (bacc[k] + back).astype(jnp.bfloat16)
            keep_store(aog.at[:, at], aog_hbm.at[:, at])
        done[k] += 1
        total = acc[q] + dot(x[:, at], block)
        if last:
            columns = pl.ds(pl.multiple_of(q * quarter, 128), quarter)
            mixed[:, columns] = (total * grow[:, columns]).astype(jnp.bfloat16)
            keep_store(mixed.at[:, columns], mixed_hbm.at[:, columns])
        else:
            acc[q] = total

    big.first(3, "l")
    big.first(3, "u")
    unit(0, "a")
    unit(0, "b")
    big.third(1)

    post.wait("rc", "c", g_got)
    g_sum[...] = gf[:, keep, :] + g_got[...].astype(jnp.float32)
    z_send[...] = g_sum[...].astype(jnp.bfloat16)
    for i, k in enumerate(ORDER):
        post.send(("rz", k), k, z_send.at[pl.ds(2 * place.far(k), 2)], z_got.at[i])

    big.second(2, "l")
    big.own_end(True)
    unit(0, "d")
    big.second(2, "u")
    big.own_end(False)
    unit(0, "e")
    unit(1, "a")
    big.third(2)
    big.second(3, "l")
    unit(1, "b")

    total = g_sum[pl.ds(2 * place.z, 2)]
    for i, k in enumerate(ORDER):
        post.wait(("rz", k), k, z_got.at[i])
        total = total + z_got[i].astype(jnp.float32)
    g_sum[pl.ds(2 * place.z, 2)] = total
    y_send[...] = g_sum[2 * place.z + 1 - place.y].astype(jnp.bfloat16)
    post.send("ry", "y", y_send, y_got)

    big.second(3, "u")
    big.end(1, True)
    unit(1, "d")
    big.end(1, False)
    unit(1, "e")
    unit(2, "a")
    post.wait("ry", "y", y_got)
    half[...] = g_sum[place.f] + y_got[...].astype(jnp.float32)
    post.send("rx", "x", half, half_got)
    big.third(3)
    unit(2, "b")
    big.end(2, True)
    unit(2, "d")
    big.end(2, False)
    unit(2, "e")

    post.wait("rx", "x", half_got)
    whole[place.c] = half[...] + half_got[...]
    post.send("rd", "c", whole.at[place.c])
    unit(3, "a", True)
    unit(3, "b", True)
    big.end(3, True)
    unit(3, "d", True)
    post.wait("rd", "c", whole.at[1 - place.c])
    for i in range(rank // 32):
        r = i * 32
        up_out[r : r + 32, :] = whole[r // hrows, r % hrows : r % hrows + 32, :] * scales[1]
    for j in range(3):
        dn_out[j * part : (j + 1) * part, :] = (
            whole[1, rank - hrows :, j * 128 : (j + 1) * 128] * scales[0]
        )
    big.end(3, False)
    unit(3, "e", True)
    post.finish()
    for store in stores:
        store.wait()


def hand_over(mixed, aog, dn, up, mixed_out, aog_out, dn_out, up_out, sems):
    copies = []
    for source, target, parts in (
        (mixed, mixed_out, 4),
        (aog, aog_out, 2),
        (dn, dn_out, 1),
        (up, up_out, 1),
    ):
        size = source.shape[0] // parts
        for i in range(parts):
            at = pl.ds(i * size, size)
            copies.append(pltpu.make_async_copy(source.at[at], target.at[at], sems.at[len(copies)]))
    for copy in copies:
        copy.start()
    for copy in copies:
        copy.wait()


def fused(x, cot, codes, amax, down, up, gate, timesteps):
    tokens, inner = x.shape
    width, rank = cot.shape[1], up.shape[0]
    rows = codes.shape[0]
    dp_count, fsdp_count = lax.axis_size("dp"), lax.axis_size("fsdp")
    per = gate.shape[0]
    shape = (timesteps.shape[0], 2 * per)
    column = lax.broadcasted_iota(jnp.int32, shape, 1)
    number = lax.axis_index("fsdp") * per + column
    half_freq = FREQ // 2
    frequency = jnp.exp(
        -math.log(10000.0) * (number % half_freq).astype(jnp.float32) / half_freq
    )
    angle = timesteps.astype(jnp.float32)[:, None] * frequency
    feat = jnp.where(number < half_freq, jnp.cos(angle), jnp.sin(angle))
    feat = jnp.where(column < per, feat, amax.astype(jnp.float32)[:, None])
    gradient_scale = (tokens * dp_count * fsdp_count) ** (-0.5)
    bf, f32 = jnp.bfloat16, jnp.float32
    quarter, hrows = width // 4, rows // 2
    vmem = pl.BlockSpec(memory_space=pltpu.VMEM)
    hbm = pl.BlockSpec(memory_space=pl.ANY)
    results = pl.pallas_call(
        functools.partial(
            kernel,
            (gradient_scale, adapter_scale_factor * gradient_scale),
            (fsdp_count * tokens, PATCHES),
        ),
        out_shape=(
            jax.ShapeDtypeStruct((tokens, width), bf),
            jax.ShapeDtypeStruct((tokens, inner), bf),
            jax.ShapeDtypeStruct((rows, rank), f32),
            jax.ShapeDtypeStruct((rank, up.shape[1]), f32),
        ),
        in_specs=[hbm, hbm] + [vmem] * 5,
        out_specs=(hbm, hbm, vmem, vmem),
        scratch_shapes=[
            pltpu.VMEM((4, inner, quarter), bf),
            pltpu.VMEM((8, rows, up.shape[1]), bf),
            pltpu.VMEM((tokens, inner), bf),
            pltpu.VMEM((tokens, width), bf),
            pltpu.VMEM((4, tokens, quarter), bf),
            pltpu.VMEM((4, tokens, quarter), f32),
            pltpu.VMEM((tokens, width), bf),
            pltpu.VMEM((tokens, inner), bf),
            pltpu.VMEM((4, tokens, 2 * rows), f32),
            pltpu.VMEM((tokens, rank), f32),
            pltpu.VMEM((rank, width), bf),
            pltpu.VMEM((inner, rank), bf),
            pltpu.VMEM((tokens, rank), bf),
            pltpu.VMEM((tokens, rank), bf),
            pltpu.VMEM((1, width), f32),
            pltpu.VMEM((timesteps.shape[0], width), f32),
            pltpu.VMEM((6, 1, width), f32),
            pltpu.VMEM((8, rows, up.shape[1]), f32),
            pltpu.VMEM((8, hrows, up.shape[1]), bf),
            pltpu.VMEM((8, hrows, up.shape[1]), bf),
            pltpu.VMEM((8, hrows, up.shape[1]), f32),
            pltpu.VMEM((8, hrows, up.shape[1]), bf),
            pltpu.VMEM((3, 2, hrows, up.shape[1]), bf),
            pltpu.VMEM((hrows, up.shape[1]), bf),
            pltpu.VMEM((hrows, up.shape[1]), bf),
            pltpu.VMEM((hrows, up.shape[1]), f32),
            pltpu.VMEM((hrows, up.shape[1]), f32),
            pltpu.VMEM((2, hrows, up.shape[1]), f32),
            pltpu.SemaphoreType.DMA((MESSAGES,)),
            pltpu.SemaphoreType.DMA((MESSAGES,)),
            pltpu.SemaphoreType.DMA((10,)),
        ],
        compiler_params=pltpu.CompilerParams(
            collective_id=0, has_side_effects=True, vmem_limit_bytes=56 * 1024 * 1024
        ),
    )(x, cot, codes, down, up, gate, feat)
    return pl.pallas_call(
        hand_over,
        out_shape=tuple(jax.ShapeDtypeStruct(r.shape, r.dtype) for r in results),
        in_specs=[hbm] * 4,
        out_specs=(hbm,) * 4,
        scratch_shapes=[pltpu.SemaphoreType.DMA((10,))],
        compiler_params=pltpu.CompilerParams(vmem_limit_bytes=60 * 1024 * 1024),
    )(*results)


def fits(mesh):
    return mesh.shape["dp"] == 4 and mesh.shape["fsdp"] == 8


def solution(mesh):
    in_specs = (
        P(("dp", "fsdp"), None),
        P(("dp", "fsdp"), None),
        P("fsdp", None),
        P("fsdp"),
        P("fsdp", None),
        P(None, "fsdp"),
        P("fsdp", None),
        P(),
    )
    out_specs = (P(("dp", "fsdp"), None), P(("dp", "fsdp"), None), P("fsdp", None), P(None, "fsdp"))
    return jax.shard_map(
        fused if fits(mesh) else per_device, mesh=mesh, in_specs=in_specs, out_specs=out_specs, check_vma=False
    )
```

```python
import functools
import math

import jax
import jax.numpy as jnp
from jax import lax
from jax.experimental import pallas as pl
from jax.experimental.pallas import tpu as pltpu
from jax.sharding import PartitionSpec as P

FREQ = 256
PATCHES = 4096


adapter_scale_factor = 0.5


def per_device(
    attention_output_rows,
    cotangent,
    quantized_weight_codes,
    shard_absolute_maximum,
    adapter_down_weight,
    adapter_up_weight,
    timestep_gate_weight,
    timesteps,
):
    row_count = attention_output_rows.shape[0]
    dp_count = lax.axis_size("dp")
    fsdp_count = lax.axis_size("fsdp")
    amax_rows = jnp.broadcast_to(shard_absolute_maximum, (quantized_weight_codes.shape[0],))
    all_codes, scales = (
        lax.all_gather(quantized_weight_codes, "fsdp", axis=0, tiled=True),
        lax.all_gather(amax_rows, "fsdp", axis=0, tiled=True),
    )
    weight = (all_codes.astype(jnp.float32) * scales.astype(jnp.float32)[:, None]).astype(
        jnp.bfloat16
    )
    down_all, gathered_up_weight, gate_all = (
        lax.all_gather(adapter_down_weight, "fsdp", axis=0, tiled=True),
        lax.all_gather(adapter_up_weight, "fsdp", axis=1, tiled=True),
        lax.all_gather(timestep_gate_weight, "fsdp", axis=0, tiled=True),
    )
    sample_index = (
        (lax.axis_index("dp") * fsdp_count + lax.axis_index("fsdp")) * row_count // PATCHES
    )
    step_value = lax.dynamic_slice_in_dim(timesteps, sample_index, 1)
    half_freq = FREQ // 2
    frequency = jnp.exp(-math.log(10000.0) * jnp.arange(half_freq, dtype=jnp.float32) / half_freq)
    phase_angle = step_value.astype(jnp.float32)[:, None] * frequency[None, :]
    features = jnp.concatenate([jnp.cos(phase_angle), jnp.sin(phase_angle)], axis=1).astype(
        jnp.bfloat16
    )
    gate_row = jnp.dot(features, gate_all, preferred_element_type=jnp.float32)
    bottleneck_activation = jnp.dot(
        attention_output_rows, down_all, preferred_element_type=jnp.float32
    ).astype(jnp.bfloat16)
    projection_output = jnp.dot(attention_output_rows, weight, preferred_element_type=jnp.float32)
    projection_output = projection_output + adapter_scale_factor * jnp.dot(
        bottleneck_activation, gathered_up_weight, preferred_element_type=jnp.float32
    )
    mixed_update = (projection_output * gate_row).astype(jnp.bfloat16)
    gated_branch_gradient = (cotangent.astype(jnp.float32) * gate_row).astype(jnp.bfloat16)
    bottleneck_gradient = (
        adapter_scale_factor
        * jnp.dot(gated_branch_gradient, gathered_up_weight.T, preferred_element_type=jnp.float32)
    ).astype(jnp.bfloat16)
    attention_output_gradient = jnp.dot(
        gated_branch_gradient, weight.T, preferred_element_type=jnp.float32
    )
    attention_output_gradient = (
        attention_output_gradient
        + jnp.dot(bottleneck_gradient, down_all.T, preferred_element_type=jnp.float32)
    ).astype(jnp.bfloat16)
    term_down = jnp.dot(
        attention_output_rows.T, bottleneck_gradient, preferred_element_type=jnp.float32
    )
    term_up = jnp.dot(
        bottleneck_activation.T, gated_branch_gradient, preferred_element_type=jnp.float32
    )
    gradient_scale_factor = (row_count * dp_count * fsdp_count) ** (-0.5)
    shard_terms = (
        lax.psum_scatter(term_down, "fsdp", scatter_dimension=0, tiled=True),
        lax.psum_scatter(term_up, "fsdp", scatter_dimension=1, tiled=True),
    )
    summed_down, reduced_up_gradient = lax.psum((shard_terms[0], shard_terms[1]), "dp")
    down_grad = summed_down * gradient_scale_factor
    scaled_up_gradient = reduced_up_gradient * (adapter_scale_factor * gradient_scale_factor)
    return (mixed_update, attention_output_gradient, down_grad, scaled_up_gradient)


MESH = pl.DeviceIdType.MESH
ORDER = (1, 3, 2)
NT = (((1,), (1,)), ((), ()))
TN = (((0,), (0,)), ((), ()))


def dot(a, b, dims=(((1,), (0,)), ((), ()))):
    return lax.dot_general(a, b, dims, preferred_element_type=jnp.float32)


class Place:
    def __init__(self):
        self.dp, self.f = lax.axis_index("dp"), lax.axis_index("fsdp")
        self.c, self.x = lax.rem(self.dp, 2), lax.rem(lax.div(self.dp, 2), 2)
        self.y, self.z = lax.rem(self.f, 2), lax.div(self.f, 2)
        self.inner = lax.rem(self.z + 1, 4) > 1

    def far(self, k):
        z = self.z
        if k == 1:
            return z + 1 - 2 * lax.rem(z, 2)
        if k == 2:
            return z + 2 - 4 * lax.div(z, 2)
        return 3 - z

    def plane(self, k):
        upper = lax.div(self.z, 2)
        if k == 1:
            return self.far(1)
        return 2 - upper if k == 2 else 3 - 3 * upper

    def device(self, way):
        if way == "c":
            return {"dp": self.dp + 1 - 2 * self.c, "fsdp": self.f}
        if way == "x":
            return {"dp": self.dp + 2 - 4 * self.x, "fsdp": self.f}
        if way == "y":
            return {"dp": self.dp, "fsdp": self.f + 1 - 2 * self.y}
        return {"dp": self.dp, "fsdp": 2 * self.far(way) + self.y}


class Post:
    def __init__(self, place, send_sems, recv_sems):
        self.place, self.ss, self.rs = place, send_sems, recv_sems
        self.index, self.sent, self.sent_inner = {}, [], []

    def _copy(self, name, way, src, dst, sender=None):
        i = self.index.setdefault(name, len(self.index))
        j = self.index.setdefault(sender or name, len(self.index))
        return pltpu.make_async_remote_copy(
            src_ref=src,
            dst_ref=dst,
            send_sem=self.ss.at[j],
            recv_sem=self.rs.at[i],
            device_id=self.place.device(way),
            device_id_type=MESH,
        )

    def send(self, name, way, src, dst=None):
        copy = self._copy(name, way, src, src if dst is None else dst)
        copy.start()
        self.sent.append(copy)

    def send_inner(self, name, way, src, sender):
        copy = self._copy(name, way, src, src, sender)
        pl.when(self.place.inner)(copy.start)
        self.sent_inner.append(copy)

    def wait(self, name, way, dst):
        self._copy(name, way, dst, dst).wait_recv()

    def finish(self):
        for copy in self.sent:
            copy.wait_send()

        @pl.when(self.place.inner)
        def _():
            for copy in self.sent_inner:
                copy.wait_send()


class Gather:
    def __init__(self, tag, post, place, piece, chain):
        self.tag, self.post, self.p, self.piece = tag, post, place, piece
        self.chain, self.far = chain, place.plane if chain else place.far

    def send(self, name, way, region):
        self.post.send((self.tag, name), way, region)

    def wait(self, name, way, region):
        self.post.wait((self.tag, name), way, region)

    def start_own(self):
        p = self.p
        for h in "lu":
            self.send(("oy", h), "y", self.piece(p.c, p.x, p.z, p.y, h))

    def part(self, zz, yy, h):
        p = self.p
        if h == "e":
            return self.piece(p.c, 1 - p.x, zz, yy, "u")
        return self.piece(p.c, p.x, zz, yy, h)

    def start(self, k, parts="lue"):
        p = self.p
        for h in parts:
            own = self.part(p.z, p.y, h)
            if self.chain and k == 3:
                self.relay(2, k, own, h, "own")
            else:
                self.send(("z", k, h), k, own)

    def relay(self, k, way, region, h, why):
        self.post.send_inner((self.tag, ("z", k, h)), way, region, (self.tag, why, k, h))

    def own_first(self, h):
        p = self.p
        got = self.piece(p.c, p.x, p.z, 1 - p.y, h)
        self.wait(("oy", h), "y", got)
        self.send(("ox", h), "x", got)
        self.send(("oc1", h), "c", got)

    def own_second(self, h):
        p = self.p
        got = self.piece(p.c, 1 - p.x, p.z, 1 - p.y, h)
        self.wait(("ox", h), "x", got)
        self.send(("oc2", h), "c", got)

    def own_end(self, same):
        p = self.p
        for h in "lu":
            if same:
                self.wait(("oc1", h), "c", self.piece(1 - p.c, p.x, p.z, 1 - p.y, h))
            else:
                self.wait(("oc2", h), "c", self.piece(1 - p.c, 1 - p.x, p.z, 1 - p.y, h))

    def first(self, k, h):
        got = self.part(self.far(k), self.p.y, h)
        self.wait(("z", k, h), k, got)
        if self.chain:
            if k == 1:
                self.relay(3, 3, got, h, "across")
            else:
                self.relay(k, 1, got, h, "out")
        if h == "e":
            if k != 1:
                self.send(("d", k, "u"), "y", got)
            self.send(("c2", k, "u"), "c", got)
            return
        if h == "l":
            self.send(("x", k), "x", got)
        self.send(("y", k, h), "y", got)
        self.send(("c1", k, h), "c", got)

    def second(self, k, h):
        p = self.p
        zz = self.far(k)
        got = self.piece(p.c, p.x, zz, 1 - p.y, h)
        self.wait(("y", k, h), "y", got)
        if h == "l" or k == 1:
            self.send(("d", k, h), "x", got)
        self.send(("c3", k, h), "c", got)
        if h == "l":
            got = self.piece(p.c, 1 - p.x, zz, p.y, h)
            self.wait(("x", k), "x", got)
            self.send(("c2", k, h), "c", got)

    def third(self, k):
        p = self.p
        for h in "lu":
            got = self.piece(p.c, 1 - p.x, self.far(k), 1 - p.y, h)
            self.wait(("d", k, h), "x" if h == "l" or k == 1 else "y", got)
            self.send(("c4", k, h), "c", got)

    def end(self, k, same):
        p = self.p
        zz, c = self.far(k), 1 - p.c
        for h in "lu":
            if same:
                self.wait(("c1", k, h), "c", self.piece(c, p.x, zz, p.y, h))
                self.wait(("c3", k, h), "c", self.piece(c, p.x, zz, 1 - p.y, h))
            else:
                self.wait(("c2", k, h), "c", self.piece(c, 1 - p.x, zz, p.y, h))
                self.wait(("c4", k, h), "c", self.piece(c, 1 - p.x, zz, 1 - p.y, h))


MESSAGES = 2 * (16 * len(ORDER) + 8) + 4 + 7 + 12


def kernel(
    scales, samples,
    x_hbm, cot_hbm, codes, down, up, gate, feat,
    mixed_hbm, aog_hbm, dn_out, up_out,
    w, pre, x, cot, bg, acc, mixed, aog, bacc, bsum, upf, downf, lr, bn, grow,
    partial, gates, gf, g_send, g_got, g_sum, z_send, z_got, y_send, y_got, half, half_got, whole,
    send_sems, recv_sems, local_sems,
):
    place = Place()
    post = Post(place, send_sems, recv_sems)
    rows, width = codes.shape
    quarter = width // 4
    shard_up = up.shape[1]
    rank = up.shape[0]
    part = down.shape[0] // 3

    load_x = pltpu.make_async_copy(x_hbm, x, local_sems.at[0])
    load_x.start()
    load_cot = pltpu.make_async_copy(cot_hbm, cot, local_sems.at[1])
    load_cot.start()

    barrier = pltpu.get_barrier_semaphore()
    ways = ("c", "x", "y") + ORDER
    for way in ways:
        pl.semaphore_signal(barrier, inc=1, device_id=place.device(way), device_id_type=MESH)

    def w_piece(c, xx, zz, yy, which):
        start, size = {"l": (0, rows // 2), "u": (rows // 2, rows // 2)}[which]
        begin = pl.multiple_of((2 * zz + yy) * rows + start, rows // 2)
        return w.at[2 * c + xx, pl.ds(begin, size)]

    def pre_piece(c, xx, zz, yy, which):
        start, size = {"l": (0, 32), "u": (32, 16)}[which]
        begin = pl.multiple_of((2 * c + xx) * 48 + start, 16)
        return pre.at[2 * zz + yy, pl.ds(begin, size)]

    big = Gather("w", post, place, w_piece, True)
    small = Gather("p", post, place, pre_piece, False)
    own = pl.ds(pl.multiple_of(place.f * rows, rows), rows)
    per = gate.shape[0]
    factor = feat[0:1, per : per + 1]

    pre[place.f, :rank, :] = up[...]
    for j in range(3):
        pre[place.f, rank:, j * 128 : (j + 1) * 128] = down[j * part : (j + 1) * part, :]
    partial[...] = dot(feat[:, :per].astype(jnp.bfloat16), gate[...])
    sample = lax.div(place.dp * samples[0], samples[1])
    gates[0] = partial[pl.ds(sample, 1), :]

    def scale(q):
        columns = pl.ds(pl.multiple_of(q * quarter, 128), quarter)
        w[q, own, :] = (codes[:, columns].astype(jnp.float32) * factor).astype(jnp.bfloat16)

    mine = 2 * place.c + place.x
    scale(mine)
    pl.semaphore_wait(barrier, len(ways))

    post.send("gy", "y", gates.at[0], gates.at[1])
    small.start_own()
    for k in ORDER:
        small.start(k)
    big.start(1, "lu")
    big.start_own()
    big.start(3, "lu")
    scale(2 * place.c + 1 - place.x)
    big.start(1, "e")
    big.start(3, "e")
    scale(2 - 2 * place.c)
    scale(3 - 2 * place.c)

    post.wait("gy", "y", gates.at[1])
    gates[2] = gates[0] + gates[1]
    for i, k in enumerate(ORDER):
        post.send(("gz", k), k, gates.at[2], gates.at[3 + i])
    for h in "lu":
        small.own_first(h)
    for k in ORDER:
        for h in "lue":
            small.first(k, h)
    big.own_first("l")
    for h in "lu":
        small.own_second(h)
    for k in ORDER:
        for h in "lu":
            small.second(k, h)
    big.first(1, "l")
    big.own_first("u")
    for k in ORDER:
        small.third(k)
    big.first(1, "u")
    big.first(1, "e")
    for i, k in enumerate(ORDER):
        post.wait(("gz", k), k, gates.at[3 + i])
    grow[...] = gates[2] + gates[3] + gates[4] + gates[5]
    for same in (True, False):
        small.own_end(same)
        for k in ORDER:
            small.end(k, same)

    @pl.loop(0, 8)
    def _(f):
        upf[:, pl.ds(pl.multiple_of(f * shard_up, 128), shard_up)] = pre[f, :rank, :]
        for j in range(3):
            to = pl.ds(pl.multiple_of(f * rows + j * part, part), part)
            downf[to, :] = pre[f, rank:, j * 128 : (j + 1) * 128]

    load_x.wait()
    load_cot.wait()
    lr[...] = dot(x[...], downf[...]).astype(jnp.bfloat16)
    bsum[...] = jnp.zeros_like(bsum)
    big.own_second("l")

    def adapter(begin, end):
        @pl.loop(begin, end)
        def _(q):
            columns = pl.ds(pl.multiple_of(q * quarter, 128), quarter)
            branch = (cot[:, columns].astype(jnp.float32) * grow[:, columns]).astype(jnp.bfloat16)
            bg[q] = branch
            ups = upf[:, columns]
            bsum[...] += dot(branch, ups, NT)
            acc[q] = 0.5 * dot(lr[...], ups)
            term = dot(lr[...], branch, TN)
            gf[2 * q, :rank, :] = term[:, :shard_up]
            gf[2 * q + 1, :rank, :] = term[:, shard_up:]

    adapter(0, 2)
    big.first(2, "l")
    big.first(2, "u")
    big.first(2, "e")
    big.own_second("u")
    big.second(1, "l")
    adapter(2, 4)
    big.second(1, "u")
    bn[...] = (0.5 * bsum[...]).astype(jnp.bfloat16)

    @pl.loop(0, 4)
    def _(zz):
        columns = pl.ds(pl.multiple_of(zz * 2 * rows, 128), 2 * rows)
        term = dot(x[:, columns], bn[...], TN)
        for b in range(6):
            gf[2 * zz + b // 3, rank:, (b % 3) * 128 : (b % 3 + 1) * 128] = term[b * part : (b + 1) * part]

    hrows = rows // 2
    keep = pl.ds(pl.multiple_of(place.c * hrows, hrows), hrows)
    give = pl.ds(pl.multiple_of((1 - place.c) * hrows, hrows), hrows)
    g_send[...] = gf[:, give, :].astype(jnp.bfloat16)
    post.send("rc", "c", g_send, g_got)

    stores = []

    def keep_store(source, target):
        store = pltpu.make_async_copy(source, target, local_sems.at[2 + len(stores)])
        store.start()
        stores.append(store)

    done = [0, 0, 0, 0]
    quarters = {
        "a": 2 * place.c + place.x,
        "b": 2 * place.c + 1 - place.x,
        "d": 2 - 2 * place.c + place.x,
        "e": 2 - 2 * place.c + 1 - place.x,
    }

    def unit(k, which, last=False):
        zz = place.plane(k) if k else place.z
        q = quarters[which]
        at = pl.ds(pl.multiple_of(zz * 2 * rows, 128), 2 * rows)
        block = w[q, at, :]
        back = dot(bg[q], block, NT)
        if done[k] == 0:
            bacc[k] = back + dot(bn[...], downf[at, :], NT)
        elif done[k] < 3:
            bacc[k] += back
        else:
            aog[:, at] = (bacc[k] + back).astype(jnp.bfloat16)
            keep_store(aog.at[:, at], aog_hbm.at[:, at])
        done[k] += 1
        total = acc[q] + dot(x[:, at], block)
        if last:
            columns = pl.ds(pl.multiple_of(q * quarter, 128), quarter)
            mixed[:, columns] = (total * grow[:, columns]).astype(jnp.bfloat16)
            keep_store(mixed.at[:, columns], mixed_hbm.at[:, columns])
        else:
            acc[q] = total

    big.first(3, "l")
    big.first(3, "u")
    big.first(3, "e")
    unit(0, "a")
    unit(0, "b")
    big.third(1)

    post.wait("rc", "c", g_got)
    g_sum[...] = gf[:, keep, :] + g_got[...].astype(jnp.float32)
    z_send[...] = g_sum[...].astype(jnp.bfloat16)
    for i, k in enumerate(ORDER):
        post.send(("rz", k), k, z_send.at[pl.ds(2 * place.far(k), 2)], z_got.at[i])

    big.second(2, "l")
    big.own_end(True)
    unit(0, "d")
    big.second(2, "u")
    big.own_end(False)
    unit(0, "e")
    unit(1, "a")
    big.third(2)
    big.second(3, "l")
    unit(1, "b")

    total = g_sum[pl.ds(2 * place.z, 2)]
    for i, k in enumerate(ORDER):
        post.wait(("rz", k), k, z_got.at[i])
        total = total + z_got[i].astype(jnp.float32)
    g_sum[pl.ds(2 * place.z, 2)] = total
    y_send[...] = g_sum[2 * place.z + 1 - place.y].astype(jnp.bfloat16)
    post.send("ry", "y", y_send, y_got)

    big.second(3, "u")
    big.end(1, True)
    unit(1, "d")
    big.end(1, False)
    unit(1, "e")
    unit(2, "a")
    post.wait("ry", "y", y_got)
    half[...] = g_sum[place.f] + y_got[...].astype(jnp.float32)
    post.send("rx", "x", half, half_got)
    big.third(3)
    unit(2, "b")
    big.end(2, True)
    unit(2, "d")
    big.end(2, False)
    unit(2, "e")

    post.wait("rx", "x", half_got)
    whole[place.c] = half[...] + half_got[...]
    post.send("rd", "c", whole.at[place.c])
    unit(3, "a", True)
    unit(3, "b", True)
    big.end(3, True)
    unit(3, "d", True)
    post.wait("rd", "c", whole.at[1 - place.c])
    for i in range(rank // 32):
        r = i * 32
        up_out[r : r + 32, :] = whole[r // hrows, r % hrows : r % hrows + 32, :] * scales[1]
    for j in range(3):
        dn_out[j * part : (j + 1) * part, :] = (
            whole[1, rank - hrows :, j * 128 : (j + 1) * 128] * scales[0]
        )
    big.end(3, False)
    unit(3, "e", True)
    post.finish()
    for store in stores:
        store.wait()


def hand_over(mixed, aog, dn, up, mixed_out, aog_out, dn_out, up_out, mixed_v, aog_v, dn_v, up_v, sems):
    steps = []
    for source, held, target, parts in (
        (mixed, mixed_v, mixed_out, 4),
        (aog, aog_v, aog_out, 2),
        (dn, dn_v, dn_out, 1),
        (up, up_v, up_out, 1),
    ):
        size = source.shape[0] // parts
        for i in range(parts):
            at, n = pl.ds(i * size, size), 2 * len(steps)
            steps.append(
                (
                    pltpu.make_async_copy(source.at[at], held.at[at], sems.at[n]),
                    pltpu.make_async_copy(held.at[at], target.at[at], sems.at[n + 1]),
                )
            )
    for fetch, _ in steps:
        fetch.start()
    for fetch, store in steps:
        fetch.wait()
        store.start()
    for _, store in steps:
        store.wait()


def fused(x, cot, codes, amax, down, up, gate, timesteps):
    tokens, inner = x.shape
    width, rank = cot.shape[1], up.shape[0]
    rows = codes.shape[0]
    dp_count, fsdp_count = lax.axis_size("dp"), lax.axis_size("fsdp")
    per = gate.shape[0]
    shape = (timesteps.shape[0], 2 * per)
    column = lax.broadcasted_iota(jnp.int32, shape, 1)
    number = lax.axis_index("fsdp") * per + column
    half_freq = FREQ // 2
    frequency = jnp.exp(
        -math.log(10000.0) * (number % half_freq).astype(jnp.float32) / half_freq
    )
    angle = timesteps.astype(jnp.float32)[:, None] * frequency
    feat = jnp.where(number < half_freq, jnp.cos(angle), jnp.sin(angle))
    feat = jnp.where(column < per, feat, amax.astype(jnp.float32)[:, None])
    gradient_scale = (tokens * dp_count * fsdp_count) ** (-0.5)
    bf, f32 = jnp.bfloat16, jnp.float32
    quarter, hrows = width // 4, rows // 2
    vmem = pl.BlockSpec(memory_space=pltpu.VMEM)
    hbm = pl.BlockSpec(memory_space=pl.ANY)
    results = pl.pallas_call(
        functools.partial(
            kernel,
            (gradient_scale, adapter_scale_factor * gradient_scale),
            (fsdp_count * tokens, PATCHES),
        ),
        out_shape=(
            jax.ShapeDtypeStruct((tokens, width), bf),
            jax.ShapeDtypeStruct((tokens, inner), bf),
            jax.ShapeDtypeStruct((rows, rank), f32),
            jax.ShapeDtypeStruct((rank, up.shape[1]), f32),
        ),
        in_specs=[hbm, hbm] + [vmem] * 5,
        out_specs=(hbm, hbm, vmem, vmem),
        scratch_shapes=[
            pltpu.VMEM((4, inner, quarter), bf),
            pltpu.VMEM((8, rows, up.shape[1]), bf),
            pltpu.VMEM((tokens, inner), bf),
            pltpu.VMEM((tokens, width), bf),
            pltpu.VMEM((4, tokens, quarter), bf),
            pltpu.VMEM((4, tokens, quarter), f32),
            pltpu.VMEM((tokens, width), bf),
            pltpu.VMEM((tokens, inner), bf),
            pltpu.VMEM((4, tokens, 2 * rows), f32),
            pltpu.VMEM((tokens, rank), f32),
            pltpu.VMEM((rank, width), bf),
            pltpu.VMEM((inner, rank), bf),
            pltpu.VMEM((tokens, rank), bf),
            pltpu.VMEM((tokens, rank), bf),
            pltpu.VMEM((1, width), f32),
            pltpu.VMEM((timesteps.shape[0], width), f32),
            pltpu.VMEM((6, 1, width), f32),
            pltpu.VMEM((8, rows, up.shape[1]), f32),
            pltpu.VMEM((8, hrows, up.shape[1]), bf),
            pltpu.VMEM((8, hrows, up.shape[1]), bf),
            pltpu.VMEM((8, hrows, up.shape[1]), f32),
            pltpu.VMEM((8, hrows, up.shape[1]), bf),
            pltpu.VMEM((3, 2, hrows, up.shape[1]), bf),
            pltpu.VMEM((hrows, up.shape[1]), bf),
            pltpu.VMEM((hrows, up.shape[1]), bf),
            pltpu.VMEM((hrows, up.shape[1]), f32),
            pltpu.VMEM((hrows, up.shape[1]), f32),
            pltpu.VMEM((2, hrows, up.shape[1]), f32),
            pltpu.SemaphoreType.DMA((MESSAGES,)),
            pltpu.SemaphoreType.DMA((MESSAGES,)),
            pltpu.SemaphoreType.DMA((10,)),
        ],
        compiler_params=pltpu.CompilerParams(
            collective_id=0, has_side_effects=True, vmem_limit_bytes=56 * 1024 * 1024
        ),
    )(x, cot, codes, down, up, gate, feat)
    return pl.pallas_call(
        hand_over,
        out_shape=tuple(jax.ShapeDtypeStruct(r.shape, r.dtype) for r in results),
        in_specs=[hbm] * 4,
        out_specs=(hbm,) * 4,
        scratch_shapes=[pltpu.VMEM(r.shape, r.dtype) for r in results]
        + [pltpu.SemaphoreType.DMA((16,))],
        compiler_params=pltpu.CompilerParams(vmem_limit_bytes=60 * 1024 * 1024),
    )(*results)


def fits(mesh):
    return mesh.shape["dp"] == 4 and mesh.shape["fsdp"] == 8


def solution(mesh):
    in_specs = (
        P(("dp", "fsdp"), None),
        P(("dp", "fsdp"), None),
        P("fsdp", None),
        P("fsdp"),
        P("fsdp", None),
        P(None, "fsdp"),
        P("fsdp", None),
        P(),
    )
    out_specs = (P(("dp", "fsdp"), None), P(("dp", "fsdp"), None), P("fsdp", None), P(None, "fsdp"))
    return jax.shard_map(
        fused if fits(mesh) else per_device, mesh=mesh, in_specs=in_specs, out_specs=out_specs, check_vma=False
    )
```

```python
import functools
import math

import jax
import jax.numpy as jnp
from jax import lax
from jax.experimental import pallas as pl
from jax.experimental.pallas import tpu as pltpu
from jax.sharding import PartitionSpec as P

FREQ = 256
PATCHES = 4096


adapter_scale_factor = 0.5


def per_device(
    attention_output_rows,
    cotangent,
    quantized_weight_codes,
    shard_absolute_maximum,
    adapter_down_weight,
    adapter_up_weight,
    timestep_gate_weight,
    timesteps,
):
    row_count = attention_output_rows.shape[0]
    dp_count = lax.axis_size("dp")
    fsdp_count = lax.axis_size("fsdp")
    amax_rows = jnp.broadcast_to(shard_absolute_maximum, (quantized_weight_codes.shape[0],))
    all_codes, scales = (
        lax.all_gather(quantized_weight_codes, "fsdp", axis=0, tiled=True),
        lax.all_gather(amax_rows, "fsdp", axis=0, tiled=True),
    )
    weight = (all_codes.astype(jnp.float32) * scales.astype(jnp.float32)[:, None]).astype(
        jnp.bfloat16
    )
    down_all, gathered_up_weight, gate_all = (
        lax.all_gather(adapter_down_weight, "fsdp", axis=0, tiled=True),
        lax.all_gather(adapter_up_weight, "fsdp", axis=1, tiled=True),
        lax.all_gather(timestep_gate_weight, "fsdp", axis=0, tiled=True),
    )
    sample_index = (
        (lax.axis_index("dp") * fsdp_count + lax.axis_index("fsdp")) * row_count // PATCHES
    )
    step_value = lax.dynamic_slice_in_dim(timesteps, sample_index, 1)
    half_freq = FREQ // 2
    frequency = jnp.exp(-math.log(10000.0) * jnp.arange(half_freq, dtype=jnp.float32) / half_freq)
    phase_angle = step_value.astype(jnp.float32)[:, None] * frequency[None, :]
    features = jnp.concatenate([jnp.cos(phase_angle), jnp.sin(phase_angle)], axis=1).astype(
        jnp.bfloat16
    )
    gate_row = jnp.dot(features, gate_all, preferred_element_type=jnp.float32)
    bottleneck_activation = jnp.dot(
        attention_output_rows, down_all, preferred_element_type=jnp.float32
    ).astype(jnp.bfloat16)
    projection_output = jnp.dot(attention_output_rows, weight, preferred_element_type=jnp.float32)
    projection_output = projection_output + adapter_scale_factor * jnp.dot(
        bottleneck_activation, gathered_up_weight, preferred_element_type=jnp.float32
    )
    mixed_update = (projection_output * gate_row).astype(jnp.bfloat16)
    gated_branch_gradient = (cotangent.astype(jnp.float32) * gate_row).astype(jnp.bfloat16)
    bottleneck_gradient = (
        adapter_scale_factor
        * jnp.dot(gated_branch_gradient, gathered_up_weight.T, preferred_element_type=jnp.float32)
    ).astype(jnp.bfloat16)
    attention_output_gradient = jnp.dot(
        gated_branch_gradient, weight.T, preferred_element_type=jnp.float32
    )
    attention_output_gradient = (
        attention_output_gradient
        + jnp.dot(bottleneck_gradient, down_all.T, preferred_element_type=jnp.float32)
    ).astype(jnp.bfloat16)
    term_down = jnp.dot(
        attention_output_rows.T, bottleneck_gradient, preferred_element_type=jnp.float32
    )
    term_up = jnp.dot(
        bottleneck_activation.T, gated_branch_gradient, preferred_element_type=jnp.float32
    )
    gradient_scale_factor = (row_count * dp_count * fsdp_count) ** (-0.5)
    shard_terms = (
        lax.psum_scatter(term_down, "fsdp", scatter_dimension=0, tiled=True),
        lax.psum_scatter(term_up, "fsdp", scatter_dimension=1, tiled=True),
    )
    summed_down, reduced_up_gradient = lax.psum((shard_terms[0], shard_terms[1]), "dp")
    down_grad = summed_down * gradient_scale_factor
    scaled_up_gradient = reduced_up_gradient * (adapter_scale_factor * gradient_scale_factor)
    return (mixed_update, attention_output_gradient, down_grad, scaled_up_gradient)


MESH = pl.DeviceIdType.MESH
ORDER = (1, 3, 2)
NT = (((1,), (1,)), ((), ()))
TN = (((0,), (0,)), ((), ()))


def dot(a, b, dims=(((1,), (0,)), ((), ()))):
    return lax.dot_general(a, b, dims, preferred_element_type=jnp.float32)


class Place:
    def __init__(self):
        self.dp, self.f = lax.axis_index("dp"), lax.axis_index("fsdp")
        self.c, self.x = lax.rem(self.dp, 2), lax.rem(lax.div(self.dp, 2), 2)
        self.y, self.z = lax.rem(self.f, 2), lax.div(self.f, 2)
        self.inner = lax.rem(self.z + 1, 4) > 1

    def far(self, k):
        z = self.z
        if k == 1:
            return z + 1 - 2 * lax.rem(z, 2)
        if k == 2:
            return z + 2 - 4 * lax.div(z, 2)
        return 3 - z

    def plane(self, k):
        upper = lax.div(self.z, 2)
        if k == 1:
            return self.far(1)
        return 2 - upper if k == 2 else 3 - 3 * upper

    def device(self, way):
        if way == "c":
            return {"dp": self.dp + 1 - 2 * self.c, "fsdp": self.f}
        if way == "x":
            return {"dp": self.dp + 2 - 4 * self.x, "fsdp": self.f}
        if way == "y":
            return {"dp": self.dp, "fsdp": self.f + 1 - 2 * self.y}
        return {"dp": self.dp, "fsdp": 2 * self.far(way) + self.y}


class Post:
    def __init__(self, place, send_sems, recv_sems):
        self.place, self.ss, self.rs = place, send_sems, recv_sems
        self.index, self.sent, self.sent_inner = {}, [], []

    def _copy(self, name, way, src, dst, sender=None):
        i = self.index.setdefault(name, len(self.index))
        j = self.index.setdefault(sender or name, len(self.index))
        return pltpu.make_async_remote_copy(
            src_ref=src,
            dst_ref=dst,
            send_sem=self.ss.at[j],
            recv_sem=self.rs.at[i],
            device_id=self.place.device(way),
            device_id_type=MESH,
        )

    def send(self, name, way, src, dst=None):
        copy = self._copy(name, way, src, src if dst is None else dst)
        copy.start()
        self.sent.append(copy)

    def send_inner(self, name, way, src, sender):
        copy = self._copy(name, way, src, src, sender)
        pl.when(self.place.inner)(copy.start)
        self.sent_inner.append(copy)

    def wait(self, name, way, dst):
        self._copy(name, way, dst, dst).wait_recv()

    def finish(self):
        for copy in self.sent:
            copy.wait_send()

        @pl.when(self.place.inner)
        def _():
            for copy in self.sent_inner:
                copy.wait_send()


class Gather:
    def __init__(self, tag, post, place, piece, chain):
        self.tag, self.post, self.p, self.piece = tag, post, place, piece
        self.chain, self.far = chain, place.plane if chain else place.far

    def send(self, name, way, region):
        self.post.send((self.tag, name), way, region)

    def wait(self, name, way, region):
        self.post.wait((self.tag, name), way, region)

    def start_own(self):
        p = self.p
        for h in "lu":
            self.send(("oy", h), "y", self.piece(p.c, p.x, p.z, p.y, h))

    def start(self, k):
        p = self.p
        for h in "lu":
            own = self.piece(p.c, p.x, p.z, p.y, h)
            if self.chain and k == 3:
                self.relay(2, k, own, h, "own")
            else:
                self.send(("z", k, h), k, own)

    def relay(self, k, way, region, h, why):
        self.post.send_inner((self.tag, ("z", k, h)), way, region, (self.tag, why, k, h))

    def own_first(self, h):
        p = self.p
        got = self.piece(p.c, p.x, p.z, 1 - p.y, h)
        self.wait(("oy", h), "y", got)
        self.send(("ox", h), "x", got)
        self.send(("oc1", h), "c", got)

    def own_second(self, h):
        p = self.p
        got = self.piece(p.c, 1 - p.x, p.z, 1 - p.y, h)
        self.wait(("ox", h), "x", got)
        self.send(("oc2", h), "c", got)

    def own_end(self, same):
        p = self.p
        for h in "lu":
            if same:
                self.wait(("oc1", h), "c", self.piece(1 - p.c, p.x, p.z, 1 - p.y, h))
            else:
                self.wait(("oc2", h), "c", self.piece(1 - p.c, 1 - p.x, p.z, 1 - p.y, h))

    def first(self, k, h):
        p = self.p
        got = self.piece(p.c, p.x, self.far(k), p.y, h)
        self.wait(("z", k, h), k, got)
        if self.chain:
            if k == 1:
                self.relay(3, 3, got, h, "across")
            else:
                self.relay(k, 1, got, h, "out")
        self.send(("x", k, h), "x", got)
        self.send(("y", k, h), "y", got)
        self.send(("c1", k, h), "c", got)

    def second(self, k, h):
        p = self.p
        zz = self.far(k)
        got = self.piece(p.c, p.x, zz, 1 - p.y, h)
        self.wait(("y", k, h), "y", got)
        if h == "u":
            self.send(("d", k, h), "x", got)
        self.send(("c3", k, h), "c", got)
        got = self.piece(p.c, 1 - p.x, zz, p.y, h)
        self.wait(("x", k, h), "x", got)
        if h == "l":
            self.send(("d", k, h), "y", got)
        self.send(("c2", k, h), "c", got)

    def third(self, k):
        p = self.p
        for h in "lu":
            got = self.piece(p.c, 1 - p.x, self.far(k), 1 - p.y, h)
            self.wait(("d", k, h), "y" if h == "l" else "x", got)
            self.send(("c4", k, h), "c", got)

    def end(self, k, same):
        p = self.p
        zz, c = self.far(k), 1 - p.c
        for h in "lu":
            if same:
                self.wait(("c1", k, h), "c", self.piece(c, p.x, zz, p.y, h))
                self.wait(("c3", k, h), "c", self.piece(c, p.x, zz, 1 - p.y, h))
            else:
                self.wait(("c2", k, h), "c", self.piece(c, 1 - p.x, zz, p.y, h))
                self.wait(("c4", k, h), "c", self.piece(c, 1 - p.x, zz, 1 - p.y, h))


MESSAGES = 2 * (16 * len(ORDER) + 8) + 4 + 7 + 8


def kernel(
    scales, samples,
    x_hbm, cot_hbm, codes, down, up, gate, feat,
    mixed_hbm, aog_hbm, dn_out, up_out,
    w, pre, x, cot, bg, acc, mixed, aog, bacc, bsum, upf, downf, lr, bn, grow,
    partial, gates, gf, g_send, g_got, g_sum, z_send, z_got, y_send, y_got, half, half_got, whole,
    send_sems, recv_sems, local_sems,
):
    place = Place()
    post = Post(place, send_sems, recv_sems)
    rows, width = codes.shape
    quarter = width // 4
    shard_up = up.shape[1]
    rank = up.shape[0]
    part = down.shape[0] // 3

    load_x = pltpu.make_async_copy(x_hbm, x, local_sems.at[0])
    load_x.start()
    load_cot = pltpu.make_async_copy(cot_hbm, cot, local_sems.at[1])
    load_cot.start()

    barrier = pltpu.get_barrier_semaphore()
    ways = ("c", "x", "y") + ORDER
    for way in ways:
        pl.semaphore_signal(barrier, inc=1, device_id=place.device(way), device_id_type=MESH)

    def w_piece(c, xx, zz, yy, which):
        start, size = {"l": (0, rows // 2), "u": (rows // 2, rows // 2)}[which]
        begin = pl.multiple_of((2 * zz + yy) * rows + start, rows // 2)
        return w.at[2 * c + xx, pl.ds(begin, size)]

    def pre_piece(c, xx, zz, yy, which):
        start, size = {"l": (0, 32), "u": (32, 16)}[which]
        begin = pl.multiple_of((2 * c + xx) * 48 + start, 16)
        return pre.at[2 * zz + yy, pl.ds(begin, size)]

    big = Gather("w", post, place, w_piece, True)
    small = Gather("p", post, place, pre_piece, False)
    own = pl.ds(pl.multiple_of(place.f * rows, rows), rows)
    per = gate.shape[0]
    factor = feat[0:1, per : per + 1]

    pre[place.f, :rank, :] = up[...]
    for j in range(3):
        pre[place.f, rank:, j * 128 : (j + 1) * 128] = down[j * part : (j + 1) * part, :]
    partial[...] = dot(feat[:, :per].astype(jnp.bfloat16), gate[...])
    sample = lax.div(place.dp * samples[0], samples[1])
    gates[0] = partial[pl.ds(sample, 1), :]

    def scale(q):
        columns = pl.ds(pl.multiple_of(q * quarter, 128), quarter)
        w[q, own, :] = (codes[:, columns].astype(jnp.float32) * factor).astype(jnp.bfloat16)

    mine = 2 * place.c + place.x
    scale(mine)
    pl.semaphore_wait(barrier, len(ways))

    post.send("gy", "y", gates.at[0], gates.at[1])
    small.start_own()
    for k in ORDER:
        small.start(k)
    for i in range(1, 4):
        scale(lax.rem(mine + i, 4))

    for h in "lu":
        small.own_first(h)
    post.wait("gy", "y", gates.at[1])
    gates[2] = gates[0] + gates[1]
    for i, k in enumerate(ORDER):
        post.send(("gz", k), k, gates.at[2], gates.at[3 + i])
    for k in ORDER:
        for h in "lu":
            small.first(k, h)
    big.start(1)
    big.start_own()
    big.start(3)
    for h in "lu":
        small.own_second(h)
    for k in ORDER:
        for h in "lu":
            small.second(k, h)
    for k in ORDER:
        small.third(k)
    for i, k in enumerate(ORDER):
        post.wait(("gz", k), k, gates.at[3 + i])
    grow[...] = gates[2] + gates[3] + gates[4] + gates[5]
    for same in (True, False):
        small.own_end(same)
        for k in ORDER:
            small.end(k, same)

    @pl.loop(0, 8)
    def _(f):
        upf[:, pl.ds(pl.multiple_of(f * shard_up, 128), shard_up)] = pre[f, :rank, :]
        for j in range(3):
            to = pl.ds(pl.multiple_of(f * rows + j * part, part), part)
            downf[to, :] = pre[f, rank:, j * 128 : (j + 1) * 128]

    big.own_first("l")
    big.first(1, "l")
    load_x.wait()
    load_cot.wait()
    lr[...] = dot(x[...], downf[...]).astype(jnp.bfloat16)
    bsum[...] = jnp.zeros_like(bsum)
    big.own_first("u")
    big.first(1, "u")

    def adapter(begin, end):
        @pl.loop(begin, end)
        def _(q):
            columns = pl.ds(pl.multiple_of(q * quarter, 128), quarter)
            branch = (cot[:, columns].astype(jnp.float32) * grow[:, columns]).astype(jnp.bfloat16)
            bg[q] = branch
            ups = upf[:, columns]
            bsum[...] += dot(branch, ups, NT)
            acc[q] = 0.5 * dot(lr[...], ups)
            term = dot(lr[...], branch, TN)
            gf[2 * q, :rank, :] = term[:, :shard_up]
            gf[2 * q + 1, :rank, :] = term[:, shard_up:]

    adapter(0, 2)
    big.own_second("l")
    big.first(2, "l")
    adapter(2, 4)
    big.first(2, "u")
    big.own_second("u")
    big.second(1, "l")
    bn[...] = (0.5 * bsum[...]).astype(jnp.bfloat16)

    @pl.loop(0, 4)
    def _(zz):
        columns = pl.ds(pl.multiple_of(zz * 2 * rows, 128), 2 * rows)
        term = dot(x[:, columns], bn[...], TN)
        for b in range(6):
            gf[2 * zz + b // 3, rank:, (b % 3) * 128 : (b % 3 + 1) * 128] = term[b * part : (b + 1) * part]

    hrows = rows // 2
    keep = pl.ds(pl.multiple_of(place.c * hrows, hrows), hrows)
    give = pl.ds(pl.multiple_of((1 - place.c) * hrows, hrows), hrows)
    g_send[...] = gf[:, give, :].astype(jnp.bfloat16)
    post.send("rc", "c", g_send, g_got)

    stores = []

    def keep_store(source, target):
        store = pltpu.make_async_copy(source, target, local_sems.at[2 + len(stores)])
        store.start()
        stores.append(store)

    done = [0, 0, 0, 0]
    quarters = {
        "a": 2 * place.c + place.x,
        "b": 2 * place.c + 1 - place.x,
        "d": 2 - 2 * place.c + place.x,
        "e": 2 - 2 * place.c + 1 - place.x,
    }

    def unit(k, which, last=False):
        zz = place.plane(k) if k else place.z
        q = quarters[which]
        at = pl.ds(pl.multiple_of(zz * 2 * rows, 128), 2 * rows)
        block = w[q, at, :]
        back = dot(bg[q], block, NT)
        if done[k] == 0:
            bacc[k] = back + dot(bn[...], downf[at, :], NT)
        elif done[k] < 3:
            bacc[k] += back
        else:
            aog[:, at] = (bacc[k] + back).astype(jnp.bfloat16)
            keep_store(aog.at[:, at], aog_hbm.at[:, at])
        done[k] += 1
        total = acc[q] + dot(x[:, at], block)
        if last:
            columns = pl.ds(pl.multiple_of(q * quarter, 128), quarter)
            mixed[:, columns] = (total * grow[:, columns]).astype(jnp.bfloat16)
            keep_store(mixed.at[:, columns], mixed_hbm.at[:, columns])
        else:
            acc[q] = total

    big.second(1, "u")
    unit(0, "a")
    big.first(3, "l")
    big.first(3, "u")
    unit(0, "b")
    big.third(1)

    post.wait("rc", "c", g_got)
    g_sum[...] = gf[:, keep, :] + g_got[...].astype(jnp.float32)
    z_send[...] = g_sum[...].astype(jnp.bfloat16)
    for i, k in enumerate(ORDER):
        post.send(("rz", k), k, z_send.at[pl.ds(2 * place.far(k), 2)], z_got.at[i])

    big.second(2, "l")
    big.own_end(True)
    unit(0, "d")
    big.second(2, "u")
    big.own_end(False)
    unit(0, "e")
    unit(1, "a")
    big.third(2)
    big.second(3, "l")
    unit(1, "b")

    total = g_sum[pl.ds(2 * place.z, 2)]
    for i, k in enumerate(ORDER):
        post.wait(("rz", k), k, z_got.at[i])
        total = total + z_got[i].astype(jnp.float32)
    g_sum[pl.ds(2 * place.z, 2)] = total
    y_send[...] = g_sum[2 * place.z + 1 - place.y].astype(jnp.bfloat16)
    post.send("ry", "y", y_send, y_got)

    big.second(3, "u")
    big.end(1, True)
    unit(1, "d")
    big.end(1, False)
    unit(1, "e")
    unit(2, "a")
    post.wait("ry", "y", y_got)
    half[...] = g_sum[place.f] + y_got[...].astype(jnp.float32)
    post.send("rx", "x", half, half_got)
    big.third(3)
    unit(2, "b")
    big.end(2, True)
    unit(2, "d")
    big.end(2, False)
    unit(2, "e")

    post.wait("rx", "x", half_got)
    whole[place.c] = half[...] + half_got[...]
    post.send("rd", "c", whole.at[place.c])
    unit(3, "a", True)
    unit(3, "b", True)
    big.end(3, True)
    unit(3, "d", True)
    post.wait("rd", "c", whole.at[1 - place.c])
    for i in range(rank // 32):
        r = i * 32
        up_out[r : r + 32, :] = whole[r // hrows, r % hrows : r % hrows + 32, :] * scales[1]
    for j in range(3):
        dn_out[j * part : (j + 1) * part, :] = (
            whole[1, rank - hrows :, j * 128 : (j + 1) * 128] * scales[0]
        )
    big.end(3, False)
    unit(3, "e", True)
    post.finish()
    for store in stores:
        store.wait()


def hand_over(mixed, aog, dn, up, mixed_out, aog_out, dn_out, up_out, mixed_v, aog_v, dn_v, up_v, sems):
    steps = []
    for source, held, target, parts in (
        (mixed, mixed_v, mixed_out, 4),
        (aog, aog_v, aog_out, 2),
        (dn, dn_v, dn_out, 1),
        (up, up_v, up_out, 1),
    ):
        size = source.shape[0] // parts
        for i in range(parts):
            at, n = pl.ds(i * size, size), 2 * len(steps)
            steps.append(
                (
                    pltpu.make_async_copy(source.at[at], held.at[at], sems.at[n]),
                    pltpu.make_async_copy(held.at[at], target.at[at], sems.at[n + 1]),
                )
            )
    for fetch, _ in steps:
        fetch.start()
    for fetch, store in steps:
        fetch.wait()
        store.start()
    for _, store in steps:
        store.wait()


def fused(x, cot, codes, amax, down, up, gate, timesteps):
    tokens, inner = x.shape
    width, rank = cot.shape[1], up.shape[0]
    rows = codes.shape[0]
    dp_count, fsdp_count = lax.axis_size("dp"), lax.axis_size("fsdp")
    per = gate.shape[0]
    shape = (timesteps.shape[0], 2 * per)
    column = lax.broadcasted_iota(jnp.int32, shape, 1)
    number = lax.axis_index("fsdp") * per + column
    half_freq = FREQ // 2
    frequency = jnp.exp(
        -math.log(10000.0) * (number % half_freq).astype(jnp.float32) / half_freq
    )
    angle = timesteps.astype(jnp.float32)[:, None] * frequency
    feat = jnp.where(number < half_freq, jnp.cos(angle), jnp.sin(angle))
    feat = jnp.where(column < per, feat, amax.astype(jnp.float32)[:, None])
    gradient_scale = (tokens * dp_count * fsdp_count) ** (-0.5)
    bf, f32 = jnp.bfloat16, jnp.float32
    quarter, hrows = width // 4, rows // 2
    vmem = pl.BlockSpec(memory_space=pltpu.VMEM)
    hbm = pl.BlockSpec(memory_space=pl.ANY)
    results = pl.pallas_call(
        functools.partial(
            kernel,
            (gradient_scale, adapter_scale_factor * gradient_scale),
            (fsdp_count * tokens, PATCHES),
        ),
        out_shape=(
            jax.ShapeDtypeStruct((tokens, width), bf),
            jax.ShapeDtypeStruct((tokens, inner), bf),
            jax.ShapeDtypeStruct((rows, rank), f32),
            jax.ShapeDtypeStruct((rank, up.shape[1]), f32),
        ),
        in_specs=[hbm, hbm] + [vmem] * 5,
        out_specs=(hbm, hbm, vmem, vmem),
        scratch_shapes=[
            pltpu.VMEM((4, inner, quarter), bf),
            pltpu.VMEM((8, rows, up.shape[1]), bf),
            pltpu.VMEM((tokens, inner), bf),
            pltpu.VMEM((tokens, width), bf),
            pltpu.VMEM((4, tokens, quarter), bf),
            pltpu.VMEM((4, tokens, quarter), f32),
            pltpu.VMEM((tokens, width), bf),
            pltpu.VMEM((tokens, inner), bf),
            pltpu.VMEM((4, tokens, 2 * rows), f32),
            pltpu.VMEM((tokens, rank), f32),
            pltpu.VMEM((rank, width), bf),
            pltpu.VMEM((inner, rank), bf),
            pltpu.VMEM((tokens, rank), bf),
            pltpu.VMEM((tokens, rank), bf),
            pltpu.VMEM((1, width), f32),
            pltpu.VMEM((timesteps.shape[0], width), f32),
            pltpu.VMEM((6, 1, width), f32),
            pltpu.VMEM((8, rows, up.shape[1]), f32),
            pltpu.VMEM((8, hrows, up.shape[1]), bf),
            pltpu.VMEM((8, hrows, up.shape[1]), bf),
            pltpu.VMEM((8, hrows, up.shape[1]), f32),
            pltpu.VMEM((8, hrows, up.shape[1]), bf),
            pltpu.VMEM((3, 2, hrows, up.shape[1]), bf),
            pltpu.VMEM((hrows, up.shape[1]), bf),
            pltpu.VMEM((hrows, up.shape[1]), bf),
            pltpu.VMEM((hrows, up.shape[1]), f32),
            pltpu.VMEM((hrows, up.shape[1]), f32),
            pltpu.VMEM((2, hrows, up.shape[1]), f32),
            pltpu.SemaphoreType.DMA((MESSAGES,)),
            pltpu.SemaphoreType.DMA((MESSAGES,)),
            pltpu.SemaphoreType.DMA((10,)),
        ],
        compiler_params=pltpu.CompilerParams(
            collective_id=0, has_side_effects=True, vmem_limit_bytes=56 * 1024 * 1024
        ),
    )(x, cot, codes, down, up, gate, feat)
    return pl.pallas_call(
        hand_over,
        out_shape=tuple(jax.ShapeDtypeStruct(r.shape, r.dtype) for r in results),
        in_specs=[hbm] * 4,
        out_specs=(hbm,) * 4,
        scratch_shapes=[pltpu.VMEM(r.shape, r.dtype) for r in results]
        + [pltpu.SemaphoreType.DMA((16,))],
        compiler_params=pltpu.CompilerParams(vmem_limit_bytes=60 * 1024 * 1024),
    )(*results)


def fits(mesh):
    return mesh.shape["dp"] == 4 and mesh.shape["fsdp"] == 8


def solution(mesh):
    in_specs = (
        P(("dp", "fsdp"), None),
        P(("dp", "fsdp"), None),
        P("fsdp", None),
        P("fsdp"),
        P("fsdp", None),
        P(None, "fsdp"),
        P("fsdp", None),
        P(),
    )
    out_specs = (P(("dp", "fsdp"), None), P(("dp", "fsdp"), None), P("fsdp", None), P(None, "fsdp"))
    return jax.shard_map(
        fused if fits(mesh) else per_device, mesh=mesh, in_specs=in_specs, out_specs=out_specs, check_vma=False
    )
```

```python
import functools
import math

import jax
import jax.numpy as jnp
from jax import lax
from jax.experimental import pallas as pl
from jax.experimental.pallas import tpu as pltpu
from jax.sharding import PartitionSpec as P

FREQ = 256
PATCHES = 4096


adapter_scale_factor = 0.5


def per_device(
    attention_output_rows,
    cotangent,
    quantized_weight_codes,
    shard_absolute_maximum,
    adapter_down_weight,
    adapter_up_weight,
    timestep_gate_weight,
    timesteps,
):
    row_count = attention_output_rows.shape[0]
    dp_count = lax.axis_size("dp")
    fsdp_count = lax.axis_size("fsdp")
    amax_rows = jnp.broadcast_to(shard_absolute_maximum, (quantized_weight_codes.shape[0],))
    all_codes, scales = (
        lax.all_gather(quantized_weight_codes, "fsdp", axis=0, tiled=True),
        lax.all_gather(amax_rows, "fsdp", axis=0, tiled=True),
    )
    weight = (all_codes.astype(jnp.float32) * scales.astype(jnp.float32)[:, None]).astype(
        jnp.bfloat16
    )
    down_all, gathered_up_weight, gate_all = (
        lax.all_gather(adapter_down_weight, "fsdp", axis=0, tiled=True),
        lax.all_gather(adapter_up_weight, "fsdp", axis=1, tiled=True),
        lax.all_gather(timestep_gate_weight, "fsdp", axis=0, tiled=True),
    )
    sample_index = (
        (lax.axis_index("dp") * fsdp_count + lax.axis_index("fsdp")) * row_count // PATCHES
    )
    step_value = lax.dynamic_slice_in_dim(timesteps, sample_index, 1)
    half_freq = FREQ // 2
    frequency = jnp.exp(-math.log(10000.0) * jnp.arange(half_freq, dtype=jnp.float32) / half_freq)
    phase_angle = step_value.astype(jnp.float32)[:, None] * frequency[None, :]
    features = jnp.concatenate([jnp.cos(phase_angle), jnp.sin(phase_angle)], axis=1).astype(
        jnp.bfloat16
    )
    gate_row = jnp.dot(features, gate_all, preferred_element_type=jnp.float32)
    bottleneck_activation = jnp.dot(
        attention_output_rows, down_all, preferred_element_type=jnp.float32
    ).astype(jnp.bfloat16)
    projection_output = jnp.dot(attention_output_rows, weight, preferred_element_type=jnp.float32)
    projection_output = projection_output + adapter_scale_factor * jnp.dot(
        bottleneck_activation, gathered_up_weight, preferred_element_type=jnp.float32
    )
    mixed_update = (projection_output * gate_row).astype(jnp.bfloat16)
    gated_branch_gradient = (cotangent.astype(jnp.float32) * gate_row).astype(jnp.bfloat16)
    bottleneck_gradient = (
        adapter_scale_factor
        * jnp.dot(gated_branch_gradient, gathered_up_weight.T, preferred_element_type=jnp.float32)
    ).astype(jnp.bfloat16)
    attention_output_gradient = jnp.dot(
        gated_branch_gradient, weight.T, preferred_element_type=jnp.float32
    )
    attention_output_gradient = (
        attention_output_gradient
        + jnp.dot(bottleneck_gradient, down_all.T, preferred_element_type=jnp.float32)
    ).astype(jnp.bfloat16)
    term_down = jnp.dot(
        attention_output_rows.T, bottleneck_gradient, preferred_element_type=jnp.float32
    )
    term_up = jnp.dot(
        bottleneck_activation.T, gated_branch_gradient, preferred_element_type=jnp.float32
    )
    gradient_scale_factor = (row_count * dp_count * fsdp_count) ** (-0.5)
    shard_terms = (
        lax.psum_scatter(term_down, "fsdp", scatter_dimension=0, tiled=True),
        lax.psum_scatter(term_up, "fsdp", scatter_dimension=1, tiled=True),
    )
    summed_down, reduced_up_gradient = lax.psum((shard_terms[0], shard_terms[1]), "dp")
    down_grad = summed_down * gradient_scale_factor
    scaled_up_gradient = reduced_up_gradient * (adapter_scale_factor * gradient_scale_factor)
    return (mixed_update, attention_output_gradient, down_grad, scaled_up_gradient)


MESH = pl.DeviceIdType.MESH
ORDER = (1, 3, 2)
NT = (((1,), (1,)), ((), ()))
TN = (((0,), (0,)), ((), ()))


def dot(a, b, dims=(((1,), (0,)), ((), ()))):
    return lax.dot_general(a, b, dims, preferred_element_type=jnp.float32)


class Place:
    def __init__(self):
        self.dp, self.f = lax.axis_index("dp"), lax.axis_index("fsdp")
        self.c, self.x = lax.rem(self.dp, 2), lax.rem(lax.div(self.dp, 2), 2)
        self.y, self.z = lax.rem(self.f, 2), lax.div(self.f, 2)

    def far(self, k):
        z = self.z
        if k == 1:
            return z + 1 - 2 * lax.rem(z, 2)
        if k == 2:
            return z + 2 - 4 * lax.div(z, 2)
        return 3 - z

    def device(self, way):
        if way == "c":
            return {"dp": self.dp + 1 - 2 * self.c, "fsdp": self.f}
        if way == "x":
            return {"dp": self.dp + 2 - 4 * self.x, "fsdp": self.f}
        if way == "y":
            return {"dp": self.dp, "fsdp": self.f + 1 - 2 * self.y}
        return {"dp": self.dp, "fsdp": 2 * self.far(way) + self.y}


class Post:
    def __init__(self, place, send_sems, recv_sems):
        self.place, self.ss, self.rs = place, send_sems, recv_sems
        self.index, self.sent = {}, []

    def _copy(self, name, way, src, dst):
        i = self.index.setdefault(name, len(self.index))
        return pltpu.make_async_remote_copy(
            src_ref=src,
            dst_ref=dst,
            send_sem=self.ss.at[i],
            recv_sem=self.rs.at[i],
            device_id=self.place.device(way),
            device_id_type=MESH,
        )

    def send(self, name, way, src, dst=None):
        copy = self._copy(name, way, src, src if dst is None else dst)
        copy.start()
        self.sent.append(copy)

    def wait(self, name, way, dst):
        self._copy(name, way, dst, dst).wait_recv()

    def finish(self):
        for copy in self.sent:
            copy.wait_send()


class Gather:
    def __init__(self, tag, post, place, piece):
        self.tag, self.post, self.p, self.piece = tag, post, place, piece

    def send(self, name, way, region):
        self.post.send((self.tag, name), way, region)

    def wait(self, name, way, region):
        self.post.wait((self.tag, name), way, region)

    def start_own(self):
        p = self.p
        for h in "lu":
            self.send(("oy", h), "y", self.piece(p.c, p.x, p.z, p.y, h))

    def start(self, k):
        p = self.p
        for h in "lu":
            self.send(("z", k, h), k, self.piece(p.c, p.x, p.z, p.y, h))

    def own_first(self, h):
        p = self.p
        got = self.piece(p.c, p.x, p.z, 1 - p.y, h)
        self.wait(("oy", h), "y", got)
        self.send(("ox", h), "x", got)
        self.send(("oc1", h), "c", got)

    def own_second(self, h):
        p = self.p
        got = self.piece(p.c, 1 - p.x, p.z, 1 - p.y, h)
        self.wait(("ox", h), "x", got)
        self.send(("oc2", h), "c", got)

    def own_end(self, same):
        p = self.p
        for h in "lu":
            if same:
                self.wait(("oc1", h), "c", self.piece(1 - p.c, p.x, p.z, 1 - p.y, h))
            else:
                self.wait(("oc2", h), "c", self.piece(1 - p.c, 1 - p.x, p.z, 1 - p.y, h))

    def first(self, k, h):
        p = self.p
        got = self.piece(p.c, p.x, p.far(k), p.y, h)
        self.wait(("z", k, h), k, got)
        self.send(("x", k, h), "x", got)
        self.send(("y", k, h), "y", got)
        self.send(("c1", k, h), "c", got)

    def second(self, k, h):
        p = self.p
        zz = p.far(k)
        got = self.piece(p.c, p.x, zz, 1 - p.y, h)
        self.wait(("y", k, h), "y", got)
        if h == "u":
            self.send(("d", k, h), "x", got)
        self.send(("c3", k, h), "c", got)
        got = self.piece(p.c, 1 - p.x, zz, p.y, h)
        self.wait(("x", k, h), "x", got)
        if h == "l":
            self.send(("d", k, h), "y", got)
        self.send(("c2", k, h), "c", got)

    def third(self, k):
        p = self.p
        for h in "lu":
            got = self.piece(p.c, 1 - p.x, p.far(k), 1 - p.y, h)
            self.wait(("d", k, h), "y" if h == "l" else "x", got)
            self.send(("c4", k, h), "c", got)

    def end(self, k, same):
        p = self.p
        zz, c = p.far(k), 1 - p.c
        for h in "lu":
            if same:
                self.wait(("c1", k, h), "c", self.piece(c, p.x, zz, p.y, h))
                self.wait(("c3", k, h), "c", self.piece(c, p.x, zz, 1 - p.y, h))
            else:
                self.wait(("c2", k, h), "c", self.piece(c, 1 - p.x, zz, p.y, h))
                self.wait(("c4", k, h), "c", self.piece(c, 1 - p.x, zz, 1 - p.y, h))


MESSAGES = 2 * (16 * len(ORDER) + 8) + 4 + 7


def kernel(
    scales, samples,
    x_hbm, cot_hbm, codes, down, up, gate, feat,
    mixed_hbm, aog_hbm, dn_out, up_out,
    w, pre, x, cot, bg, acc, mixed, aog, bacc, bsum, upf, downf, lr, bn, grow,
    partial, gates, gf, g_send, g_got, g_sum, z_send, z_got, y_send, y_got, half, half_got, whole,
    send_sems, recv_sems, local_sems,
):
    place = Place()
    post = Post(place, send_sems, recv_sems)
    rows, width = codes.shape
    quarter = width // 4
    shard_up = up.shape[1]
    rank = up.shape[0]
    part = down.shape[0] // 3

    load_x = pltpu.make_async_copy(x_hbm, x, local_sems.at[0])
    load_x.start()
    load_cot = pltpu.make_async_copy(cot_hbm, cot, local_sems.at[1])
    load_cot.start()

    barrier = pltpu.get_barrier_semaphore()
    ways = ("c", "x", "y") + ORDER
    for way in ways:
        pl.semaphore_signal(barrier, inc=1, device_id=place.device(way), device_id_type=MESH)

    def w_piece(c, xx, zz, yy, which):
        start, size = {"l": (0, rows // 2), "u": (rows // 2, rows // 2)}[which]
        begin = pl.multiple_of((2 * zz + yy) * rows + start, rows // 2)
        return w.at[2 * c + xx, pl.ds(begin, size)]

    def pre_piece(c, xx, zz, yy, which):
        start, size = {"l": (0, 32), "u": (32, 16)}[which]
        begin = pl.multiple_of((2 * c + xx) * 48 + start, 16)
        return pre.at[2 * zz + yy, pl.ds(begin, size)]

    big = Gather("w", post, place, w_piece)
    small = Gather("p", post, place, pre_piece)
    own = pl.ds(pl.multiple_of(place.f * rows, rows), rows)
    per = gate.shape[0]
    factor = feat[0:1, per : per + 1]

    pre[place.f, :rank, :] = up[...]
    for j in range(3):
        pre[place.f, rank:, j * 128 : (j + 1) * 128] = down[j * part : (j + 1) * part, :]
    partial[...] = dot(feat[:, :per].astype(jnp.bfloat16), gate[...])
    sample = lax.div(place.dp * samples[0], samples[1])
    gates[0] = partial[pl.ds(sample, 1), :]

    def scale(q):
        columns = pl.ds(pl.multiple_of(q * quarter, 128), quarter)
        w[q, own, :] = (codes[:, columns].astype(jnp.float32) * factor).astype(jnp.bfloat16)

    mine = 2 * place.c + place.x
    scale(mine)
    pl.semaphore_wait(barrier, len(ways))

    post.send("gy", "y", gates.at[0], gates.at[1])
    small.start_own()
    for k in ORDER:
        small.start(k)
    big.start(1)
    big.start_own()
    big.start(3)
    for i in range(1, 4):
        scale(lax.rem(mine + i, 4))

    post.wait("gy", "y", gates.at[1])
    gates[2] = gates[0] + gates[1]
    for i, k in enumerate(ORDER):
        post.send(("gz", k), k, gates.at[2], gates.at[3 + i])
    for h in "lu":
        small.own_first(h)
    for k in ORDER:
        for h in "lu":
            small.first(k, h)
    big.own_first("l")
    for h in "lu":
        small.own_second(h)
    for k in ORDER:
        for h in "lu":
            small.second(k, h)
    big.own_first("u")
    for k in ORDER:
        small.third(k)
    for i, k in enumerate(ORDER):
        post.wait(("gz", k), k, gates.at[3 + i])
    grow[...] = gates[2] + gates[3] + gates[4] + gates[5]
    for same in (True, False):
        small.own_end(same)
        for k in ORDER:
            small.end(k, same)

    @pl.loop(0, 8)
    def _(f):
        upf[:, pl.ds(pl.multiple_of(f * shard_up, 128), shard_up)] = pre[f, :rank, :]
        for j in range(3):
            to = pl.ds(pl.multiple_of(f * rows + j * part, part), part)
            downf[to, :] = pre[f, rank:, j * 128 : (j + 1) * 128]

    load_x.wait()
    load_cot.wait()
    big.first(1, "l")
    lr[...] = dot(x[...], downf[...]).astype(jnp.bfloat16)
    bsum[...] = jnp.zeros_like(bsum)
    big.first(1, "u")
    big.start(2)

    def adapter(begin, end):
        @pl.loop(begin, end)
        def _(q):
            columns = pl.ds(pl.multiple_of(q * quarter, 128), quarter)
            branch = (cot[:, columns].astype(jnp.float32) * grow[:, columns]).astype(jnp.bfloat16)
            bg[q] = branch
            ups = upf[:, columns]
            bsum[...] += dot(branch, ups, NT)
            acc[q] = 0.5 * dot(lr[...], ups)
            term = dot(lr[...], branch, TN)
            gf[2 * q, :rank, :] = term[:, :shard_up]
            gf[2 * q + 1, :rank, :] = term[:, shard_up:]

    adapter(0, 2)
    big.own_second("l")
    big.own_second("u")
    adapter(2, 4)
    big.second(1, "l")
    bn[...] = (0.5 * bsum[...]).astype(jnp.bfloat16)

    @pl.loop(0, 4)
    def _(zz):
        columns = pl.ds(pl.multiple_of(zz * 2 * rows, 128), 2 * rows)
        term = dot(x[:, columns], bn[...], TN)
        for b in range(6):
            gf[2 * zz + b // 3, rank:, (b % 3) * 128 : (b % 3 + 1) * 128] = term[b * part : (b + 1) * part]

    hrows = rows // 2
    keep = pl.ds(pl.multiple_of(place.c * hrows, hrows), hrows)
    give = pl.ds(pl.multiple_of((1 - place.c) * hrows, hrows), hrows)
    g_send[...] = gf[:, give, :].astype(jnp.bfloat16)
    post.send("rc", "c", g_send, g_got)

    stores = []

    def keep_store(source, target):
        store = pltpu.make_async_copy(source, target, local_sems.at[2 + len(stores)])
        store.start()
        stores.append(store)

    done = [0, 0, 0, 0]
    quarters = {
        "a": 2 * place.c + place.x,
        "b": 2 * place.c + 1 - place.x,
        "d": 2 - 2 * place.c + place.x,
        "e": 2 - 2 * place.c + 1 - place.x,
    }

    def unit(k, which, last=False):
        zz = place.far(k) if k else place.z
        q = quarters[which]
        at = pl.ds(pl.multiple_of(zz * 2 * rows, 128), 2 * rows)
        block = w[q, at, :]
        back = dot(bg[q], block, NT)
        if done[k] == 0:
            bacc[k] = back + dot(bn[...], downf[at, :], NT)
        elif done[k] < 3:
            bacc[k] += back
        else:
            aog[:, at] = (bacc[k] + back).astype(jnp.bfloat16)
            keep_store(aog.at[:, at], aog_hbm.at[:, at])
        done[k] += 1
        total = acc[q] + dot(x[:, at], block)
        if last:
            columns = pl.ds(pl.multiple_of(q * quarter, 128), quarter)
            mixed[:, columns] = (total * grow[:, columns]).astype(jnp.bfloat16)
            keep_store(mixed.at[:, columns], mixed_hbm.at[:, columns])
        else:
            acc[q] = total

    big.first(3, "l")
    big.first(3, "u")
    big.second(1, "u")
    unit(0, "a")
    unit(0, "b")
    big.third(1)

    post.wait("rc", "c", g_got)
    g_sum[...] = gf[:, keep, :] + g_got[...].astype(jnp.float32)
    z_send[...] = g_sum[...].astype(jnp.bfloat16)
    for i, k in enumerate(ORDER):
        post.send(("rz", k), k, z_send.at[pl.ds(2 * place.far(k), 2)], z_got.at[i])

    big.first(2, "l")
    big.second(3, "l")
    big.first(2, "u")
    big.second(3, "u")
    big.own_end(True)
    unit(0, "d")
    big.own_end(False)
    unit(0, "e")
    big.third(3)
    unit(1, "a")
    big.second(2, "l")
    unit(1, "b")

    total = g_sum[pl.ds(2 * place.z, 2)]
    for i, k in enumerate(ORDER):
        post.wait(("rz", k), k, z_got.at[i])
        total = total + z_got[i].astype(jnp.float32)
    g_sum[pl.ds(2 * place.z, 2)] = total
    y_send[...] = g_sum[2 * place.z + 1 - place.y].astype(jnp.bfloat16)
    post.send("ry", "y", y_send, y_got)

    big.second(2, "u")
    big.end(1, True)
    unit(1, "d")
    big.end(1, False)
    unit(1, "e")
    unit(3, "a")
    post.wait("ry", "y", y_got)
    half[...] = g_sum[place.f] + y_got[...].astype(jnp.float32)
    post.send("rx", "x", half, half_got)
    unit(3, "b")
    big.third(2)
    unit(2, "a", True)
    big.end(3, True)
    unit(3, "d")
    big.end(3, False)
    unit(3, "e")

    post.wait("rx", "x", half_got)
    whole[place.c] = half[...] + half_got[...]
    post.send("rd", "c", whole.at[place.c])
    big.end(2, True)
    unit(2, "d", True)
    unit(2, "b", True)
    post.wait("rd", "c", whole.at[1 - place.c])
    for i in range(rank // 32):
        r = i * 32
        up_out[r : r + 32, :] = whole[r // hrows, r % hrows : r % hrows + 32, :] * scales[1]
    for j in range(3):
        dn_out[j * part : (j + 1) * part, :] = (
            whole[1, rank - hrows :, j * 128 : (j + 1) * 128] * scales[0]
        )
    big.end(2, False)
    unit(2, "e", True)
    post.finish()
    for store in stores:
        store.wait()


def hand_over(mixed, aog, dn, up, mixed_out, aog_out, dn_out, up_out, mixed_v, aog_v, dn_v, up_v, sems):
    steps = []
    for source, held, target, parts in (
        (mixed, mixed_v, mixed_out, 4),
        (aog, aog_v, aog_out, 2),
        (dn, dn_v, dn_out, 1),
        (up, up_v, up_out, 1),
    ):
        size = source.shape[0] // parts
        for i in range(parts):
            at, n = pl.ds(i * size, size), 2 * len(steps)
            steps.append(
                (
                    pltpu.make_async_copy(source.at[at], held.at[at], sems.at[n]),
                    pltpu.make_async_copy(held.at[at], target.at[at], sems.at[n + 1]),
                )
            )
    for fetch, _ in steps:
        fetch.start()
    for fetch, store in steps:
        fetch.wait()
        store.start()
    for _, store in steps:
        store.wait()


def fused(x, cot, codes, amax, down, up, gate, timesteps):
    tokens, inner = x.shape
    width, rank = cot.shape[1], up.shape[0]
    rows = codes.shape[0]
    dp_count, fsdp_count = lax.axis_size("dp"), lax.axis_size("fsdp")
    per = gate.shape[0]
    shape = (timesteps.shape[0], 2 * per)
    column = lax.broadcasted_iota(jnp.int32, shape, 1)
    number = lax.axis_index("fsdp") * per + column
    half_freq = FREQ // 2
    frequency = jnp.exp(
        -math.log(10000.0) * (number % half_freq).astype(jnp.float32) / half_freq
    )
    angle = timesteps.astype(jnp.float32)[:, None] * frequency
    feat = jnp.where(number < half_freq, jnp.cos(angle), jnp.sin(angle))
    feat = jnp.where(column < per, feat, amax.astype(jnp.float32)[:, None])
    gradient_scale = (tokens * dp_count * fsdp_count) ** (-0.5)
    bf, f32 = jnp.bfloat16, jnp.float32
    quarter, hrows = width // 4, rows // 2
    vmem = pl.BlockSpec(memory_space=pltpu.VMEM)
    hbm = pl.BlockSpec(memory_space=pl.ANY)
    results = pl.pallas_call(
        functools.partial(
            kernel,
            (gradient_scale, adapter_scale_factor * gradient_scale),
            (fsdp_count * tokens, PATCHES),
        ),
        out_shape=(
            jax.ShapeDtypeStruct((tokens, width), bf),
            jax.ShapeDtypeStruct((tokens, inner), bf),
            jax.ShapeDtypeStruct((rows, rank), f32),
            jax.ShapeDtypeStruct((rank, up.shape[1]), f32),
        ),
        in_specs=[hbm, hbm] + [vmem] * 5,
        out_specs=(hbm, hbm, vmem, vmem),
        scratch_shapes=[
            pltpu.VMEM((4, inner, quarter), bf),
            pltpu.VMEM((8, rows, up.shape[1]), bf),
            pltpu.VMEM((tokens, inner), bf),
            pltpu.VMEM((tokens, width), bf),
            pltpu.VMEM((4, tokens, quarter), bf),
            pltpu.VMEM((4, tokens, quarter), f32),
            pltpu.VMEM((tokens, width), bf),
            pltpu.VMEM((tokens, inner), bf),
            pltpu.VMEM((4, tokens, 2 * rows), f32),
            pltpu.VMEM((tokens, rank), f32),
            pltpu.VMEM((rank, width), bf),
            pltpu.VMEM((inner, rank), bf),
            pltpu.VMEM((tokens, rank), bf),
            pltpu.VMEM((tokens, rank), bf),
            pltpu.VMEM((1, width), f32),
            pltpu.VMEM((timesteps.shape[0], width), f32),
            pltpu.VMEM((6, 1, width), f32),
            pltpu.VMEM((8, rows, up.shape[1]), f32),
            pltpu.VMEM((8, hrows, up.shape[1]), bf),
            pltpu.VMEM((8, hrows, up.shape[1]), bf),
            pltpu.VMEM((8, hrows, up.shape[1]), f32),
            pltpu.VMEM((8, hrows, up.shape[1]), bf),
            pltpu.VMEM((3, 2, hrows, up.shape[1]), bf),
            pltpu.VMEM((hrows, up.shape[1]), bf),
            pltpu.VMEM((hrows, up.shape[1]), bf),
            pltpu.VMEM((hrows, up.shape[1]), f32),
            pltpu.VMEM((hrows, up.shape[1]), f32),
            pltpu.VMEM((2, hrows, up.shape[1]), f32),
            pltpu.SemaphoreType.DMA((MESSAGES,)),
            pltpu.SemaphoreType.DMA((MESSAGES,)),
            pltpu.SemaphoreType.DMA((10,)),
        ],
        compiler_params=pltpu.CompilerParams(
            collective_id=0, has_side_effects=True, vmem_limit_bytes=56 * 1024 * 1024
        ),
    )(x, cot, codes, down, up, gate, feat)
    return pl.pallas_call(
        hand_over,
        out_shape=tuple(jax.ShapeDtypeStruct(r.shape, r.dtype) for r in results),
        in_specs=[hbm] * 4,
        out_specs=(hbm,) * 4,
        scratch_shapes=[pltpu.VMEM(r.shape, r.dtype) for r in results]
        + [pltpu.SemaphoreType.DMA((16,))],
        compiler_params=pltpu.CompilerParams(vmem_limit_bytes=60 * 1024 * 1024),
    )(*results)


def fits(mesh):
    return mesh.shape["dp"] == 4 and mesh.shape["fsdp"] == 8


def solution(mesh):
    in_specs = (
        P(("dp", "fsdp"), None),
        P(("dp", "fsdp"), None),
        P("fsdp", None),
        P("fsdp"),
        P("fsdp", None),
        P(None, "fsdp"),
        P("fsdp", None),
        P(),
    )
    out_specs = (P(("dp", "fsdp"), None), P(("dp", "fsdp"), None), P("fsdp", None), P(None, "fsdp"))
    return jax.shard_map(
        fused if fits(mesh) else per_device, mesh=mesh, in_specs=in_specs, out_specs=out_specs, check_vma=False
    )
```
